32 devices in a mesh: ens: 2 (over x), tile: 16 (over z, y, core).
Axes of the slice: x: 2, y: 2, z: 4, core: 2. Of those that a mesh axis runs over, the one named last changes fastest.
Arguments:
- adjoint_in: float32 [16, 72, 256, 128], P('ens', None, 'tile'), parts along dimension 0, may hold values from -6 to 6
- east_courant: float32 [144, 256, 128], P('ens', 'tile'), parts along dimension 0, may hold values from -0.25 to 0.25
- north_courant: float32 [144, 256, 128], P('ens', 'tile'), parts along dimension 0, may hold values from -0.25 to 0.25
- level_mix: bfloat16 [72, 72], replicated, may hold values from -0.05 to 1, as said below
- avg_kernel: bfloat16 [144, 16384], P('ens', 'tile'), parts along dimension 0, may hold values from 0.19921875 to 1.796875
- pixel_weight: bfloat16 [16, 16384], P('ens', 'tile'), parts along dimension 0, may hold values from -6 to 6
- pixel_owner: int32 [16384, 2], P('tile', 'ens'), parts along dimension 1, may hold values from 0 to 15; in each aligned block of 1024 rows (0 to 1023, 1024 to 2047, ...) at most 256 rows name the same one
- pixel_column: int32 [2, 16384], P('ens', 'tile'), parts along dimension 0, may hold values from 0 to 2047
Outputs:
- adjoint_out: float32 [16, 72, 256, 128], P('ens', None, 'tile'), parts along dimension 0
The draws below stay inside these ranges and needn't reach their ends.
There are 2 independent parts, one for each index of `ens`. The reference program is written for one: setup_inputs(seed, part) draws one part's arguments, and reference() takes and returns one part's arrays. A program takes and returns all parts, laid end to end along the dimension named above; an argument that names none is the same for every part. Nothing has to cross between parts.
Inputs may be any that keep to these rules, and one draw needn't show every extreme that they name: `pixel_owner`: of the 1024 pixels of one device, at most 256 name the same tile; in every draw some device sends exactly 256 to some tile. `level_mix`: diagonally dominant: each row's off-diagonal magnitudes sum to less than its diagonal entry, which lies in 0.6 to 1.
All inputs are finite; a program needn't handle non-finite values.
Results may differ from the reference program's by a relative error of at most 0.0052.
Values may be sent and summed in bfloat16 or wider, within the bound.
No kernel may reach another device: no remote copies, remote signals or barrier semaphores. Data moves between devices by JAX's collectives and lax.ppermute only.
A program may use at most 128 MiB of HBM per device.

```python
import math
import jax
import jax.numpy as jnp
import numpy as np
from jax import lax

NT = 8
L = 72
STEPS = 4
NLAT = 128
PIX_DEV = 1024
COLS_DEV = 2048
LON = 256
PIX_TOT = 16384
CAP = 256
N_TILE = 16


def draw_level_mix(key, part):
    key = jax.random.fold_in(key, 11)
    first_key, second_key = jax.random.split(key)
    diagonal = jax.random.uniform(first_key, (L,), jnp.float32, 0.7, 1.0)
    spread = jax.random.uniform(second_key, (L, L), jnp.float32, -1.0, 1.0) * (0.6 / L)
    identity = jnp.eye(L, dtype=jnp.float32)
    return (identity * diagonal[:, None] + spread * (1.0 - identity)).astype(jnp.bfloat16)


def set_ends(values, key, smallest, top_value):
    longest = values.shape.index(max(values.shape))
    spots = []
    for shift in (0, 1):
        where = [jax.random.randint(jax.random.fold_in(key, axis), (), 0, length) for axis, length in enumerate(values.shape)]
        where[longest] = (where[longest] + shift) % values.shape[longest]
        spots.append(tuple(where))
    return values.at[spots[0]].set(smallest).at[spots[1]].set(top_value)


def level_of(key, extent, pieces, least, top_value):
    factor_of, own = 1.0, jax.random.fold_in(key, 6)
    for dim, parts in pieces:
        steps = jnp.exp(jax.random.uniform(jax.random.fold_in(own, dim), (parts,), jnp.float32, least / len(pieces), top_value / len(pieces)))
        factor_of = factor_of * jnp.repeat(steps, extent[dim] // parts).reshape([-1 if axis == dim else 1 for axis in range(len(extent))])
    return factor_of


def shared_out(stream_key, own, number, rows, number_of, top, bound, slope):
    ranking = jax.random.permutation(stream_key, number_of)
    crowded, usual = portions_of(number_of, rows * top, bound, slope, True), portions_of(number_of, rows * top, bound, slope, False)
    places = jnp.arange(number_of)

    def named(sizes, offset_by):
        used = int((sizes > 0).sum())
        fixed = max(1, used // 4)
        shifted = fixed + (places - fixed + offset_by * (used - fixed)) % max(1, number_of - fixed)
        return jnp.zeros((number_of,), jnp.int32).at[ranking[jnp.where(places < fixed, places, shifted)]].set(jnp.asarray(sizes, jnp.int32))

    sizes = jnp.where(number % 4 == 0, named(crowded, number // 4), named(usual, number - number // 4 - 1))
    mixed = jax.random.permutation(jax.random.fold_in(own, 3), number_of)
    giver, receiver = mixed[0:number_of // 2 * 2:2], mixed[1:number_of // 2 * 2:2]
    slack = jnp.minimum(sizes[giver] - 1, bound - sizes[receiver]) // 2
    slack = jnp.where((giver == ranking[0]) | (receiver == ranking[0]) | (sizes[receiver] == 0), 0, jnp.maximum(slack, 0))
    shifted = jax.random.randint(jax.random.fold_in(own, 4), (number_of // 2,), 0, 1 << 20) % (slack + 1)
    sizes = sizes.at[giver].add(-shifted).at[receiver].add(shifted)
    items = jnp.searchsorted(jnp.cumsum(sizes), jnp.arange(rows * top), side="right").astype(jnp.int32)
    table = items.reshape(top, rows).T
    table = table[jax.random.permutation(jax.random.fold_in(own, 1), rows)]
    offset_by = jax.random.randint(jax.random.fold_in(own, 2), (rows, 1), 0, top)
    return jnp.take_along_axis(table, (jnp.arange(top)[None, :] + offset_by) % top, axis=1)


def portions_of(number_of, total, reach, skew, full):
    loads = [(1 << 20) // math.isqrt(rank ** skew) + 1 for rank in range(1, number_of + 1)]
    largest = reach if full else min(reach, max(-(-total // number_of), total * loads[0] // sum(loads)))
    least = 1 if total - largest >= number_of - 1 else 0
    holding, surplus = [largest] + [least] * (number_of - 1), total - largest - least * (number_of - 1)
    while surplus > 0:
        free = [i for i in range(1, number_of) if holding[i] < largest] or [i for i in range(1, number_of) if holding[i] < reach]
        mass, remaining = sum([loads[i] for i in free]), surplus
        for i in free:
            addition = min(reach - holding[i], max(1, remaining * loads[i] // mass), surplus)
            holding[i] = holding[i] + addition
            surplus = surplus - addition
    return np.array(holding)


def bell_draw(stream_key, shape, deviation, bound, pieces=(), held_as=jnp.bfloat16):
    values = deviation * jax.random.normal(stream_key, shape, jnp.float32)
    if pieces:
        values = values * level_of(stream_key, shape, pieces, -0.22, 0.18)
    return jnp.clip(values, -bound, bound).astype(held_as)


def setup_inputs(seed: int = 0, part: int = 0) -> dict:
    arg_keys = jax.random.split(jax.random.key(seed), 9)
    part_splits = jax.random.split(jax.random.fold_in(arg_keys[8], part), 9)
    adjoint_in = bell_draw(part_splits[0], (NT, L, LON, NLAT), 1.0, 6.0, ((2, 16),), jnp.float32)
    east_courant = jnp.clip(jax.random.uniform(part_splits[1], (L, LON, NLAT), jnp.float32, -0.25, 0.25) * level_of(part_splits[1], (L, LON, NLAT), ((1, 16),), -0.4, 0.0), -0.25, 0.25)
    north_courant = jnp.clip(jax.random.uniform(part_splits[2], (L, LON, NLAT), jnp.float32, -0.25, 0.25) * level_of(part_splits[2], (L, LON, NLAT), ((1, 16),), -0.4, 0.0), -0.25, 0.25)
    level_mix = draw_level_mix(jax.random.fold_in(arg_keys[8], 71), part)
    avg_kernel = jnp.clip(0.19921875 + 1.5976562 * jax.random.uniform(part_splits[4], (L, PIX_TOT), jnp.float32) ** level_of(part_splits[4], (L, PIX_TOT), ((1, 16),), -0.2, 0.2), 0.19921875, 1.796875).astype(jnp.bfloat16)
    pixel_weight = bell_draw(part_splits[5], (NT, PIX_TOT), 1.0, 6.0, ((1, 16),))
    pixel_owner_keys = jax.random.split(jax.random.fold_in(part_splits[6], 1), PIX_TOT // PIX_DEV)
    pixel_owner_turns = jax.random.permutation(jax.random.fold_in(part_splits[6], 3), PIX_TOT // PIX_DEV)
    pixel_owner = jax.vmap(lambda own, number: shared_out(jax.random.fold_in(part_splits[6], 2), own, number, PIX_DEV, N_TILE, 1, CAP, 2))(pixel_owner_keys, pixel_owner_turns).reshape((PIX_TOT, 1))
    pixel_column = set_ends(jax.random.randint(part_splits[7], (1, PIX_TOT), 0, COLS_DEV), jax.random.fold_in(part_splits[7], 1), 0, COLS_DEV - 1).astype(jnp.int32)
    return {"adjoint_in": adjoint_in, "east_courant": east_courant, "north_courant": north_courant, "level_mix": level_mix, "avg_kernel": avg_kernel, "pixel_weight": pixel_weight, "pixel_owner": pixel_owner, "pixel_column": pixel_column}


def mix_levels(field, level_mix):
    rounded = lax.optimization_barrier(field.astype(jnp.bfloat16))
    return jnp.einsum('lm,tlxy->tmxy', level_mix.astype(jnp.float32), rounded.astype(jnp.float32), precision=lax.Precision.HIGHEST)


def transport(extended, east_face, west_face, north_face):
    centre = extended[:, :, 1:-1]
    east_value = extended[:, :, 2:]
    west_value = extended[:, :, :-2]
    zeros_row = jnp.zeros_like(centre[..., :1])
    north_value = jnp.concatenate([centre[..., 1:], zeros_row], axis=-1)
    south_value = jnp.concatenate([zeros_row, centre[..., :-1]], axis=-1)
    south_face = jnp.concatenate([jnp.zeros_like(north_face[..., :1]), north_face[..., :-1]], axis=-1)
    result = centre + jnp.maximum(east_face, 0.0) * (east_value - centre)
    result = result + jnp.minimum(west_face, 0.0) * (centre - west_value)
    result = result + jnp.maximum(north_face, 0.0) * (north_value - centre)
    return result + jnp.minimum(south_face, 0.0) * (centre - south_value)


def reference(adjoint_in, east_courant, north_courant, level_mix, avg_kernel, pixel_weight, pixel_owner, pixel_column):
    latitude = jnp.arange(NLAT, dtype=jnp.int32)
    north_face = north_courant * (latitude < NLAT - 1).astype(jnp.float32)
    west_face = jnp.roll(east_courant, 1, axis=1)

    def adjoint_step(field):
        mixed_field = mix_levels(field, level_mix)
        extended = jnp.concatenate([mixed_field[:, :, -1:], mixed_field, mixed_field[:, :, :1]], axis=2)
        return transport(extended, east_courant, west_face, north_face)

    weighted = (pixel_weight.astype(jnp.float32)[:, None, :] * avg_kernel.astype(jnp.float32)[None, :, :]).astype(jnp.bfloat16)
    weighted = weighted.reshape(NT * L, PIX_TOT)
    target = (pixel_owner[:, 0] * COLS_DEV + pixel_column[0]).astype(jnp.int32)
    forcing = jax.ops.segment_sum(weighted.astype(jnp.float32).T, target, num_segments=LON * NLAT)
    forcing = forcing.T.reshape(NT, L, LON, NLAT)
    field = adjoint_in
    for turn_index in range(STEPS // 2):
        field = adjoint_step(field)
    field = field + forcing
    for turn_index in range(STEPS // 2):
        field = adjoint_step(field)
    return field
```

```python
import functools

import jax
import jax.numpy as jnp
from jax import lax
from jax.experimental import pallas as pl
from jax.experimental.pallas import tpu as pltpu
from jax.sharding import PartitionSpec as P

F32 = jnp.float32
BF16 = jnp.bfloat16
GROUP = 2
HALO = 2
VMEM = 56 * 1024 * 1024


def params(**more):
    return pltpu.CompilerParams(vmem_limit_bytes=VMEM, **more)


def nt_dot(a, b):
    return lax.dot_general(a, b, (((1,), (1,)), ((), ())), preferred_element_type=F32)


def rows16(row):
    return jnp.broadcast_to(row, (16, row.shape[1])).astype(BF16)


def stacked(block, count):
    return jnp.concatenate([block] * count, axis=0)


def pack_kernel(kernel_ref, weight_ref, owner_ref, column_ref, out_ref, *, tiles, capacity, lat):
    levels, pixels = kernel_ref.shape
    column = column_ref[...]
    lon_row = (column // lat).astype(F32)
    lat_row = (column % lat).astype(F32)
    line = lax.broadcasted_iota(jnp.int32, (8, pixels), 0)
    place = jnp.where(line == 0, lon_row, jnp.where(line == 1, lat_row, 0.0))
    payload = jnp.concatenate(
        [kernel_ref[...].astype(F32), weight_ref[...].astype(F32), place], axis=0
    ).astype(BF16)
    owner = owner_ref[...]
    block = min(256, pixels)
    upto = (
        lax.broadcasted_iota(jnp.int32, (block, block), 0)
        <= lax.broadcasted_iota(jnp.int32, (block, block), 1)
    ).astype(F32).astype(BF16)
    carry = jnp.zeros((tiles, 1), F32)
    ranks = []
    for start in range(0, pixels, block):
        named = owner[:, start : start + block] == lax.broadcasted_iota(
            jnp.int32, (tiles, block), 0
        )
        counts = (
            jnp.dot(named.astype(F32).astype(BF16), upto, preferred_element_type=F32) + carry
        )
        carry = counts[:, block - 1 : block]
        ranks.append(jnp.where(named, counts - 1.0, -1.0))
    ranks = jnp.concatenate(ranks, axis=1)
    slot = lax.broadcasted_iota(jnp.int32, (capacity, pixels), 0).astype(F32).astype(BF16)
    for tile in range(tiles):
        rank = stacked(rows16(ranks[tile : tile + 1, :]), capacity // 16)
        chosen = jnp.where(slot == rank, jnp.ones_like(slot), jnp.zeros_like(slot))
        out_ref[tile] = nt_dot(payload, chosen).astype(BF16)


def edge_kernel(field_ref, east_ref, north_ref, fwd_ref, bwd_ref, *, lon, levels):
    step = pl.program_id(0)
    rows = field_ref.shape[0] // lon
    total = rows * pl.num_programs(0)

    def column(ref, x, count):
        return ref[pl.ds(x, count, stride=lon), :].astype(BF16)

    for c in range(HALO):
        at = pl.ds(pl.multiple_of(c * total + step * rows, 16), rows)
        fwd_ref[at, :] = column(field_ref, lon - HALO + c, rows)
        bwd_ref[at, :] = column(field_ref, c, rows)

    @pl.when(step == 0)
    def _():
        def put(out, place, ref, x):
            spot = HALO * total + place * (levels + 8)
            value = ref[pl.ds(x, levels, stride=lon), :]
            value = jnp.concatenate([value, jnp.zeros((8, value.shape[1]), F32)], axis=0)
            out[spot : spot + levels + 8, :] = value.astype(BF16)

        put(fwd_ref, 0, east_ref, lon - 2)
        put(fwd_ref, 1, east_ref, lon - 1)
        put(fwd_ref, 2, north_ref, lon - 1)
        put(bwd_ref, 0, east_ref, 0)
        put(bwd_ref, 1, north_ref, 0)


def fill_coefs(east_ref, north_ref, fwd_ref, bwd_ref, coef_ref, lon, levels, total):
    lat = east_ref.shape[1]
    base = HALO * total

    def far(ref, place):
        spot = base + place * (levels + 8)
        return ref[spot : spot + levels + 8, :].astype(F32)[:levels]

    def own(ref, x):
        return ref[pl.ds(x, levels, stride=lon), :]

    def east(e):
        if e < HALO:
            return far(fwd_ref, e)
        return own(east_ref, e - HALO) if e < lon + HALO else far(bwd_ref, 0)

    def north(e):
        if e < HALO:
            return far(fwd_ref, 2)
        return own(north_ref, e - HALO) if e < lon + HALO else far(bwd_ref, 1)

    lane = lax.broadcasted_iota(jnp.int32, (levels, lat), 1)
    for e in range(1, lon + 2 * HALO - 1):
        at = slice(e * lat, (e + 1) * lat)
        face = jnp.where(lane < lat - 1, north(e), 0.0)
        to_east = jnp.maximum(east(e), 0.0)
        to_west = jnp.minimum(east(e - 1), 0.0)
        to_north = jnp.maximum(face, 0.0)
        to_south = pltpu.roll(jnp.minimum(face, 0.0), 1, 1)
        coef_ref[0, :, at] = (1.0 - to_east) + to_west + (to_south - to_north)
        coef_ref[1, :, at] = to_east
        coef_ref[2, :, at] = -to_west
        coef_ref[3, :, at] = to_north
        coef_ref[4, :, at] = -to_south


def stencil(mixed_ref, coef_ref, e, lat, levels, emit):
    rows = mixed_ref.shape[0]
    here = pl.ds(pl.multiple_of(e * lat, lat), lat)
    right = pl.ds(pl.multiple_of(e * lat + lat, lat), lat)
    left = pl.ds(pl.multiple_of(e * lat - lat, lat), lat)
    for k in range(0, rows, levels):
        part = slice(k, k + levels)
        centre = mixed_ref[part, here]
        value = coef_ref[0, :, here] * centre
        value = value + coef_ref[1, :, here] * mixed_ref[part, right]
        value = value + coef_ref[2, :, here] * mixed_ref[part, left]
        value = value + coef_ref[3, :, here] * pltpu.roll(centre, lat - 1, 1)
        value = value + coef_ref[4, :, here] * pltpu.roll(centre, 1, 1)
        emit(k, value)


def two_steps(mix_ref, field_ref, mixed_ref, hold_ref, coef_ref, lon, lat, levels, put):
    whole = lon + 2 * HALO
    mixed_ref[...] = jnp.dot(mix_ref[...], field_ref[...], preferred_element_type=F32)

    def first(e, carry):
        here = pl.ds(pl.multiple_of(e * lat, lat), lat)

        def emit(k, value):
            hold_ref[k : k + levels, :] = value

        stencil(mixed_ref, coef_ref, e, lat, levels, emit)
        field_ref[:, here] = hold_ref[...].astype(BF16)
        return carry

    lax.fori_loop(1, whole - 1, first, 0)
    inner = slice(lat, (whole - 1) * lat)
    mixed_ref[:, inner] = jnp.dot(mix_ref[...], field_ref[:, inner], preferred_element_type=F32)

    def second(e, carry):
        stencil(mixed_ref, coef_ref, e, lat, levels, functools.partial(put, e))
        return carry

    lax.fori_loop(HALO, whole - HALO, second, 0)


def first_half_kernel(
    mix_ref, east_ref, north_ref, fwd_ref, bwd_ref, in_ref, out_ref,
    coef_ref, field_ref, mixed_ref, hold_ref, *, lon, levels, total,
):
    step = pl.program_id(0)
    lat = in_ref.shape[1]
    rows = in_ref.shape[0] // lon

    @pl.when(step == 0)
    def _():
        fill_coefs(east_ref, north_ref, fwd_ref, bwd_ref, coef_ref, lon, levels, total)

    for c in range(HALO):
        at = pl.ds(pl.multiple_of(c * total + step * rows, 16), rows)
        field_ref[:, c * lat : (c + 1) * lat] = fwd_ref[at, :]
        e = lon + HALO + c
        field_ref[:, e * lat : (e + 1) * lat] = bwd_ref[at, :]
    for x in range(lon):
        value = in_ref[pl.ds(x, rows, stride=lon), :]
        field_ref[:, (x + HALO) * lat : (x + HALO + 1) * lat] = value.astype(BF16)

    def put(e, k, value):
        out_ref[k : k + levels, pl.ds(pl.multiple_of((e - HALO) * lat, lat), lat)] = value

    two_steps(mix_ref, field_ref, mixed_ref, hold_ref, coef_ref, lon, lat, levels, put)


def second_half_kernel(
    mix_ref, east_ref, north_ref, fwd_ref, bwd_ref, far_w_ref, own_w_ref, inner_ref, own_e_ref,
    far_e_ref, out_ref, coef_ref, field_ref, mixed_ref, hold_ref, *, lon, levels, total,
):
    lat = out_ref.shape[1]
    rows = out_ref.shape[0] // lon

    @pl.when(pl.program_id(0) == 0)
    def _():
        fill_coefs(east_ref, north_ref, fwd_ref, bwd_ref, coef_ref, lon, levels, total)

    spot = 0
    for ref in (far_w_ref, own_w_ref, inner_ref, own_e_ref, far_e_ref):
        width = ref.shape[-1]
        field_ref[:, spot : spot + width] = ref[...]
        spot = spot + width

    def put(e, k, value):
        out_ref[pl.ds(k * lon + e - HALO, levels, stride=lon), :] = value

    two_steps(mix_ref, field_ref, mixed_ref, hold_ref, coef_ref, lon, lat, levels, put)


def forcing_kernel(got_ref, field_ref, out_ref, weighted_ref, place_ref, *, lat, levels, tracers, pair):
    tiles, _, capacity = got_ref.shape
    step = pl.program_id(0)

    @pl.when(step == 0)
    def _():
        for tile in range(tiles):
            at = slice(tile * capacity, (tile + 1) * capacity)
            got = got_ref[tile].astype(F32)
            kernel = got[:levels]
            for t in range(0, tracers, GROUP):
                parts = [
                    kernel * got[levels + j : levels + j + 1, :] for j in range(t, t + GROUP)
                ]
                weighted_ref[t * levels : (t + GROUP) * levels, at] = jnp.concatenate(
                    parts, axis=0
                ).astype(BF16)
            spot = levels + tracers
            column = got[spot : spot + 1, :] * lat + got[spot + 1 : spot + 2, :]
            place_ref[:, at] = jnp.broadcast_to(column, (8, capacity))

    cells = field_ref.shape[1]
    slots = tiles * capacity
    offset = (pair(step) * cells).astype(F32)
    key = rows16(place_ref[0:1, :] - offset)
    cell = lax.broadcasted_iota(jnp.int32, (cells, slots), 0).astype(F32).astype(BF16)
    hit = cell == stacked(key, cells // 16)
    one_hot = jnp.where(hit, jnp.ones_like(cell), jnp.zeros_like(cell))
    total = nt_dot(weighted_ref[...], one_hot)
    out_ref[...] = (field_ref[...] + total).astype(BF16)


def per_device(
    adjoint_in,
    east_courant,
    north_courant,
    level_mix,
    avg_kernel,
    pixel_weight,
    pixel_owner,
    pixel_column,
):
    tracers, levels, lon, lat = adjoint_in.shape
    pixels = avg_kernel.shape[1]
    tiles = lax.axis_size("tile")
    capacity = 4 * pixels // tiles
    slots = tiles * capacity
    total = tracers * levels
    steps = tracers // GROUP
    rows = GROUP * levels
    ring = [(i, (i + 1) % tiles) for i in range(tiles)]
    back = [((i + 1) % tiles, i) for i in range(tiles)]

    field = adjoint_in.reshape(total * lon, lat)
    east = east_courant.reshape(levels * lon, lat)
    north = north_courant.reshape(levels * lon, lat)
    mix = jnp.kron(jnp.eye(GROUP, dtype=BF16), level_mix.T)

    height = levels + tracers + 8
    payload = pl.pallas_call(
        functools.partial(pack_kernel, tiles=tiles, capacity=capacity, lat=lat),
        out_shape=jax.ShapeDtypeStruct((tiles, height, capacity), BF16),
        compiler_params=params(),
        name="pack",
    )(avg_kernel, pixel_weight, pixel_owner.reshape(1, pixels), pixel_column)
    got = lax.all_to_all(payload, "tile", split_axis=0, concat_axis=0, tiled=True)

    fwd_rows = HALO * total + 3 * (levels + 8)
    bwd_rows = HALO * total + 2 * (levels + 8)
    whole = lambda *shape: pl.BlockSpec(shape, lambda i: (0,) * len(shape))
    fwd, bwd = pl.pallas_call(
        functools.partial(edge_kernel, lon=lon, levels=levels),
        grid=(steps,),
        in_specs=[
            pl.BlockSpec((rows * lon, lat), lambda i: (i, 0)),
            whole(levels * lon, lat),
            whole(levels * lon, lat),
        ],
        out_specs=[whole(fwd_rows, lat), whole(bwd_rows, lat)],
        out_shape=[
            jax.ShapeDtypeStruct((fwd_rows, lat), BF16),
            jax.ShapeDtypeStruct((bwd_rows, lat), BF16),
        ],
        compiler_params=params(),
        name="edges",
    )(field, east, north)
    fwd = lax.ppermute(fwd, "tile", ring)
    bwd = lax.ppermute(bwd, "tile", back)

    span = (lon + 2 * HALO) * lat
    scratch = [
        pltpu.VMEM((5, levels, span), F32),
        pltpu.VMEM((rows, span), BF16),
        pltpu.VMEM((rows, span), F32),
        pltpu.VMEM((rows, lat), F32),
    ]
    common_specs = [
        whole(rows, rows),
        whole(levels * lon, lat),
        whole(levels * lon, lat),
        whole(fwd_rows, lat),
        whole(bwd_rows, lat),
    ]
    middle = pl.pallas_call(
        functools.partial(first_half_kernel, lon=lon, levels=levels, total=total),
        grid=(steps,),
        in_specs=common_specs + [pl.BlockSpec((rows * lon, lat), lambda i: (i, 0))],
        out_specs=pl.BlockSpec((rows, lon * lat), lambda i: (i, 0)),
        out_shape=jax.ShapeDtypeStruct((total, lon * lat), F32),
        scratch_shapes=scratch,
        compiler_params=params(),
        name="first_half",
    )(mix, east, north, fwd, bwd, field)

    cells = HALO * lat
    pairs = lon // HALO

    def forced(name, count, pair):
        return pl.pallas_call(
            functools.partial(
                forcing_kernel, lat=lat, levels=levels, tracers=tracers, pair=pair
            ),
            grid=(count,),
            in_specs=[
                whole(tiles, height, capacity),
                pl.BlockSpec((total, cells), lambda i: (0, pair(i))),
            ],
            out_specs=pl.BlockSpec((total, cells), lambda i: (0, i)),
            out_shape=jax.ShapeDtypeStruct((total, count * cells), BF16),
            scratch_shapes=[pltpu.VMEM((total, slots), BF16), pltpu.VMEM((8, slots), F32)],
            compiler_params=params(),
            name=name,
        )(got, middle)

    rim = forced("forcing_rim", 2, lambda i: i * (pairs - 1))
    own_w, own_e = rim[:, :cells], rim[:, cells:]
    far_w = lax.ppermute(own_e, "tile", ring)
    far_e = lax.ppermute(own_w, "tile", back)
    inner = forced("forcing_inner", pairs - 2, lambda i: i + 1)

    strip = lambda width: pl.BlockSpec((rows, width), lambda i: (i, 0))
    out = pl.pallas_call(
        functools.partial(second_half_kernel, lon=lon, levels=levels, total=total),
        grid=(steps,),
        in_specs=common_specs
        + [strip(cells), strip(cells), strip((pairs - 2) * cells), strip(cells), strip(cells)],
        out_specs=pl.BlockSpec((rows * lon, lat), lambda i: (i, 0)),
        out_shape=jax.ShapeDtypeStruct((total * lon, lat), F32),
        scratch_shapes=scratch,
        compiler_params=params(),
        name="second_half",
    )(mix, east, north, fwd, bwd, far_w, own_w, inner, own_e, far_e)
    return out.reshape(tracers, levels, lon, lat)


def solution(mesh):
    in_specs = (
        P("ens", None, "tile", None),
        P("ens", "tile", None),
        P("ens", "tile", None),
        P(),
        P("ens", "tile"),
        P("ens", "tile"),
        P("tile", "ens"),
        P("ens", "tile"),
    )
    out_specs = P("ens", None, "tile", None)
    return jax.shard_map(
        per_device, mesh=mesh, in_specs=in_specs, out_specs=out_specs, check_vma=False
    )
```

```python
import functools

import jax
import jax.numpy as jnp
from jax import lax
from jax.experimental import pallas as pl
from jax.experimental.pallas import tpu as pltpu
from jax.sharding import PartitionSpec as P

F32 = jnp.float32
BF16 = jnp.bfloat16
GROUP = 2
HALO = 2
VMEM = 56 * 1024 * 1024


def params(**more):
    return pltpu.CompilerParams(vmem_limit_bytes=VMEM, **more)


def nt_dot(a, b):
    return lax.dot_general(a, b, (((1,), (1,)), ((), ())), preferred_element_type=F32)


def rows16(row):
    return jnp.broadcast_to(row, (16, row.shape[1])).astype(BF16)


def stacked(block, count):
    return jnp.concatenate([block] * count, axis=0)


def pack_kernel(kernel_ref, weight_ref, owner_ref, column_ref, out_ref, *, tiles, capacity, lat):
    levels, pixels = kernel_ref.shape
    column = column_ref[...]
    lon_row = (column // lat).astype(F32)
    lat_row = (column % lat).astype(F32)
    line = lax.broadcasted_iota(jnp.int32, (8, pixels), 0)
    place = jnp.where(line == 0, lon_row, jnp.where(line == 1, lat_row, 0.0))
    payload = jnp.concatenate(
        [kernel_ref[...].astype(F32), weight_ref[...].astype(F32), place], axis=0
    ).astype(BF16)
    owner = owner_ref[...]
    block = min(256, pixels)
    upto = (
        lax.broadcasted_iota(jnp.int32, (block, block), 0)
        <= lax.broadcasted_iota(jnp.int32, (block, block), 1)
    ).astype(F32).astype(BF16)
    carry = jnp.zeros((tiles, 1), F32)
    ranks = []
    for start in range(0, pixels, block):
        named = owner[:, start : start + block] == lax.broadcasted_iota(
            jnp.int32, (tiles, block), 0
        )
        counts = (
            jnp.dot(named.astype(F32).astype(BF16), upto, preferred_element_type=F32) + carry
        )
        carry = counts[:, block - 1 : block]
        ranks.append(jnp.where(named, counts - 1.0, -1.0))
    ranks = jnp.concatenate(ranks, axis=1)
    slot = lax.broadcasted_iota(jnp.int32, (capacity, pixels), 0).astype(F32).astype(BF16)
    for tile in range(tiles):
        rank = stacked(rows16(ranks[tile : tile + 1, :]), capacity // 16)
        chosen = jnp.where(slot == rank, jnp.ones_like(slot), jnp.zeros_like(slot))
        out_ref[tile] = nt_dot(payload, chosen).astype(BF16)


def both(ref, block, x, lon, levels):
    parts = [
        ref[pl.ds((t * levels + block * 8) * lon + x, 8, stride=lon), :] for t in range(GROUP)
    ]
    return jnp.concatenate(parts, axis=0).astype(BF16)


def edge_kernel(field_ref, east_ref, north_ref, fwd_ref, bwd_ref, *, lon, levels):
    step = pl.program_id(0)
    rows = field_ref.shape[0] // lon
    total = rows * pl.num_programs(0)
    for c in range(HALO):
        for block in range(levels // 8):
            spot = c * total + step * rows + block * 8 * GROUP
            at = pl.ds(pl.multiple_of(spot, 16), 8 * GROUP)
            fwd_ref[at, :] = both(field_ref, block, lon - HALO + c, lon, levels)
            bwd_ref[at, :] = both(field_ref, block, c, lon, levels)

    @pl.when(step == 0)
    def _():
        def put(out, place, ref, x):
            spot = HALO * total + place * (levels + 8)
            value = ref[pl.ds(x, levels, stride=lon), :]
            value = jnp.concatenate([value, jnp.zeros((8, value.shape[1]), F32)], axis=0)
            out[spot : spot + levels + 8, :] = value.astype(BF16)

        put(fwd_ref, 0, east_ref, lon - 2)
        put(fwd_ref, 1, east_ref, lon - 1)
        put(fwd_ref, 2, north_ref, lon - 1)
        put(bwd_ref, 0, east_ref, 0)
        put(bwd_ref, 1, north_ref, 0)


def fill_coefs(east_ref, north_ref, edges, coef_ref, columns, lon, levels, total):
    lat = east_ref.shape[1]
    base = HALO * total

    def far(ref, place):
        spot = base + place * (levels + 8)
        return ref[spot : spot + levels + 8, :].astype(F32)[:levels]

    def own(ref, x):
        return ref[pl.ds(x, levels, stride=lon), :]

    def east(x):
        if x < 0:
            return far(edges[0], x + HALO)
        return own(east_ref, x) if x < lon else far(edges[1], 0)

    def north(x):
        if x < 0:
            return far(edges[0], 2)
        return own(north_ref, x) if x < lon else far(edges[1], 1)

    lane = lax.broadcasted_iota(jnp.int32, (levels, lat), 1)
    for i, x in enumerate(columns):
        at = slice(i * lat, (i + 1) * lat)
        face = jnp.where(lane < lat - 1, north(x), 0.0)
        to_east = jnp.maximum(east(x), 0.0)
        to_west = jnp.minimum(east(x - 1), 0.0)
        to_north = jnp.maximum(face, 0.0)
        to_south = pltpu.roll(jnp.minimum(face, 0.0), 1, 1)
        coef_ref[0, :, at] = (1.0 - to_east) + to_west + (to_south - to_north)
        coef_ref[1, :, at] = to_east
        coef_ref[2, :, at] = -to_west
        coef_ref[3, :, at] = to_north
        coef_ref[4, :, at] = -to_south


def stencil(mixed_ref, coef_ref, start, count, coef_start, lat, levels, emit):
    def column(e):
        return slice(e * lat, (e + 1) * lat)

    for block in range(levels // 8):
        lines = slice(block * 8, block * 8 + 8)
        tracer_rows = [
            slice(block * 8 * GROUP + 8 * t, block * 8 * GROUP + 8 * t + 8) for t in range(GROUP)
        ]
        left = [mixed_ref[r, column(start - 1)] for r in tracer_rows]
        centre = [mixed_ref[r, column(start)] for r in tracer_rows]
        for e in range(start, start + count):
            at = column(coef_start + e - start)
            factor = [coef_ref[j, lines, at] for j in range(5)]
            values = []
            for t, r in enumerate(tracer_rows):
                right = mixed_ref[r, column(e + 1)]
                value = (factor[0] * centre[t] + factor[1] * right) + (
                    factor[2] * left[t] + factor[3] * pltpu.roll(centre[t], lat - 1, 1)
                )
                values.append(value + factor[4] * pltpu.roll(centre[t], 1, 1))
                left[t], centre[t] = centre[t], right
            emit(block, e, values)


def two_steps(mix_ref, field_ref, mixed_ref, coef_ref, start, count, coef_start, lat, levels, put):
    def mix(lo, hi):
        for e in range(lo, hi, 2):
            at = slice(e * lat, (e + 2) * lat)
            mixed_ref[:, at] = jnp.dot(mix_ref[...], field_ref[:, at], preferred_element_type=F32)

    def keep(block, e, values):
        at = slice(block * 8 * GROUP, (block + 1) * 8 * GROUP)
        field_ref[at, e * lat : (e + 1) * lat] = jnp.concatenate(values, axis=0).astype(BF16)

    mix(start, start + count)
    stencil(mixed_ref, coef_ref, start + 1, count - 2, coef_start, lat, levels, keep)
    mix(start + 1, start + count - 1)
    stencil(mixed_ref, coef_ref, start + 2, count - 4, coef_start + 1, lat, levels, put)


def inner_kernel(
    mix_ref, east_ref, north_ref, in_ref, out_ref, near_ref, coef_ref, field_ref, mixed_ref,
    *, lon, levels,
):
    lat = in_ref.shape[1]

    @pl.when(pl.program_id(0) == 0)
    def _():
        fill_coefs(east_ref, north_ref, None, coef_ref, range(1, lon - 1), lon, levels, 0)

    for x in range(lon):
        for block in range(levels // 8):
            at = slice(block * 8 * GROUP, (block + 1) * 8 * GROUP)
            field_ref[at, x * lat : (x + 1) * lat] = both(in_ref, block, x, lon, levels)
    side = 2 * HALO * lat
    near_ref[:, :side] = field_ref[:, :side]
    near_ref[:, side:] = field_ref[:, lon * lat - side :]

    def put(block, e, values):
        for t, value in enumerate(values):
            row = block * 8 * GROUP + 8 * t
            out_ref[row : row + 8, (e - HALO) * lat : (e - HALO + 1) * lat] = value

    two_steps(mix_ref, field_ref, mixed_ref, coef_ref, 0, lon, 0, lat, levels, put)


def rim_kernel(
    mix_ref, east_ref, north_ref, fwd_ref, bwd_ref, near_ref, out_ref, coef_ref, field_ref,
    mixed_ref, *, lon, levels, total,
):
    step = pl.program_id(0)
    lat = fwd_ref.shape[1]
    rows = near_ref.shape[0]
    wide = 3 * HALO

    @pl.when(step == 0)
    def _():
        columns = list(range(1 - HALO, HALO + 1)) + list(range(lon - HALO - 1, lon + HALO - 1))
        fill_coefs(
            east_ref, north_ref, (fwd_ref, bwd_ref), coef_ref, columns, lon, levels, total
        )

    for c in range(HALO):
        at = pl.ds(pl.multiple_of(c * total + step * rows, 16), rows)
        field_ref[:, c * lat : (c + 1) * lat] = fwd_ref[at, :]
        e = wide + 2 * HALO + c
        field_ref[:, e * lat : (e + 1) * lat] = bwd_ref[at, :]
    side = 2 * HALO * lat
    field_ref[:, HALO * lat : HALO * lat + side] = near_ref[:, :side]
    field_ref[:, wide * lat : wide * lat + side] = near_ref[:, side:]
    for half in range(2):
        start = half * wide

        def put(block, e, values):
            spot = (e - start - HALO + half * HALO) * lat
            for t, value in enumerate(values):
                row = block * 8 * GROUP + 8 * t
                out_ref[row : row + 8, spot : spot + lat] = value

        two_steps(
            mix_ref, field_ref, mixed_ref, coef_ref, start, wide, half * 2 * HALO, lat, levels, put
        )


def second_half_kernel(
    mix_ref, east_ref, north_ref, fwd_ref, bwd_ref, far_w_ref, own_w_ref, inner_ref, own_e_ref,
    far_e_ref, out_ref, coef_ref, field_ref, mixed_ref, *, lon, levels, total,
):
    lat = out_ref.shape[1]

    @pl.when(pl.program_id(0) == 0)
    def _():
        columns = range(1 - HALO, lon + HALO - 1)
        fill_coefs(
            east_ref, north_ref, (fwd_ref, bwd_ref), coef_ref, columns, lon, levels, total
        )

    spot = 0
    for ref in (far_w_ref, own_w_ref, inner_ref, own_e_ref, far_e_ref):
        width = ref.shape[-1]
        field_ref[:, spot : spot + width] = ref[...]
        spot = spot + width

    def put(block, e, values):
        for t, value in enumerate(values):
            first = (t * levels + block * 8) * lon + e - HALO
            out_ref[pl.ds(first, 8, stride=lon), :] = value

    two_steps(
        mix_ref, field_ref, mixed_ref, coef_ref, 0, lon + 2 * HALO, 0, lat, levels, put
    )


def forcing(got_ref, field, weighted_ref, place_ref, step, pair, *, lat, levels, tracers):
    tiles, _, capacity = got_ref.shape

    @pl.when(step == 0)
    def _():
        for tile in range(tiles):
            at = slice(tile * capacity, (tile + 1) * capacity)
            got = got_ref[tile].astype(F32)
            row = 0
            for t in range(0, tracers, GROUP):
                for block in range(0, levels, 8):
                    kernel = got[block : block + 8]
                    parts = [
                        kernel * got[levels + j : levels + j + 1, :] for j in range(t, t + GROUP)
                    ]
                    value = jnp.concatenate(parts, axis=0).astype(BF16)
                    weighted_ref[row : row + 8 * GROUP, at] = value
                    row = row + 8 * GROUP
            spot = levels + tracers
            column = got[spot : spot + 1, :] * lat + got[spot + 1 : spot + 2, :]
            place_ref[:, at] = jnp.broadcast_to(column, (8, capacity))

    cells = HALO * lat
    slots = tiles * capacity
    key = rows16(place_ref[0:1, :] - (pair * cells).astype(F32))
    cell = lax.broadcasted_iota(jnp.int32, (cells, slots), 0).astype(F32).astype(BF16)
    hit = cell == stacked(key, cells // 16)
    one_hot = jnp.where(hit, jnp.ones_like(cell), jnp.zeros_like(cell))
    return (field + nt_dot(weighted_ref[...], one_hot)).astype(BF16)


def forcing_inner_kernel(got_ref, field_ref, out_ref, weighted_ref, place_ref, **sizes):
    step = pl.program_id(0)
    out_ref[...] = forcing(got_ref, field_ref[...], weighted_ref, place_ref, step, step + 1, **sizes)


def forcing_rim_kernel(
    got_ref, field_ref, west_ref, east_ref, weighted_ref, place_ref, *, pairs, **sizes
):
    step = pl.program_id(0)
    value = forcing(
        got_ref, field_ref[...], weighted_ref, place_ref, step, step * (pairs - 1), **sizes
    )

    @pl.when(step == 0)
    def _():
        west_ref[...] = value

    @pl.when(step == 1)
    def _():
        east_ref[...] = value


def per_device(
    adjoint_in,
    east_courant,
    north_courant,
    level_mix,
    avg_kernel,
    pixel_weight,
    pixel_owner,
    pixel_column,
):
    tracers, levels, lon, lat = adjoint_in.shape
    pixels = avg_kernel.shape[1]
    tiles = lax.axis_size("tile")
    capacity = 4 * pixels // tiles
    slots = tiles * capacity
    total = tracers * levels
    steps = tracers // GROUP
    rows = GROUP * levels
    ring = [(i, (i + 1) % tiles) for i in range(tiles)]
    back = [((i + 1) % tiles, i) for i in range(tiles)]

    field = adjoint_in.reshape(total * lon, lat)
    east = east_courant.reshape(levels * lon, lat)
    north = north_courant.reshape(levels * lon, lat)
    blocks = level_mix.T.reshape(levels // 8, 1, 8, levels // 8, 1, 8)
    same = jnp.eye(GROUP, dtype=BF16).reshape(1, GROUP, 1, 1, GROUP, 1)
    mix = (blocks * same).reshape(rows, rows)

    height = levels + tracers + 8
    payload = pl.pallas_call(
        functools.partial(pack_kernel, tiles=tiles, capacity=capacity, lat=lat),
        out_shape=jax.ShapeDtypeStruct((tiles, height, capacity), BF16),
        compiler_params=params(),
        name="pack",
    )(avg_kernel, pixel_weight, pixel_owner.reshape(1, pixels), pixel_column)
    got = lax.all_to_all(payload, "tile", split_axis=0, concat_axis=0, tiled=True)

    fwd_rows = HALO * total + 3 * (levels + 8)
    bwd_rows = HALO * total + 2 * (levels + 8)
    whole = lambda *shape: pl.BlockSpec(shape, lambda i: (0,) * len(shape))
    fwd, bwd = pl.pallas_call(
        functools.partial(edge_kernel, lon=lon, levels=levels),
        grid=(steps,),
        in_specs=[
            pl.BlockSpec((rows * lon, lat), lambda i: (i, 0)),
            whole(levels * lon, lat),
            whole(levels * lon, lat),
        ],
        out_specs=[whole(fwd_rows, lat), whole(bwd_rows, lat)],
        out_shape=[
            jax.ShapeDtypeStruct((fwd_rows, lat), BF16),
            jax.ShapeDtypeStruct((bwd_rows, lat), BF16),
        ],
        compiler_params=params(),
        name="edges",
    )(field, east, north)
    fwd = lax.ppermute(fwd, "tile", ring)
    bwd = lax.ppermute(bwd, "tile", back)

    def scratch(columns, coefs):
        return [
            pltpu.VMEM((5, levels, coefs * lat), F32),
            pltpu.VMEM((rows, columns * lat), BF16),
            pltpu.VMEM((rows, columns * lat), F32),
        ]

    strip = lambda width: pl.BlockSpec((rows, width), lambda i: (i, 0))
    cells = HALO * lat
    pairs = lon // HALO
    fixed_specs = [whole(rows, rows), whole(levels * lon, lat), whole(levels * lon, lat)]
    edge_specs = [whole(fwd_rows, lat), whole(bwd_rows, lat)]
    inner_width = (lon - 2 * HALO) * lat
    middle, near = pl.pallas_call(
        functools.partial(inner_kernel, lon=lon, levels=levels),
        grid=(steps,),
        in_specs=fixed_specs + [pl.BlockSpec((rows * lon, lat), lambda i: (i, 0))],
        out_specs=[strip(inner_width), strip(4 * cells)],
        out_shape=[
            jax.ShapeDtypeStruct((total, inner_width), F32),
            jax.ShapeDtypeStruct((total, 4 * cells), BF16),
        ],
        scratch_shapes=scratch(lon, lon - 2),
        compiler_params=params(),
        name="first_half_inner",
    )(mix, east, north, field)
    rim = pl.pallas_call(
        functools.partial(rim_kernel, lon=lon, levels=levels, total=total),
        grid=(steps,),
        in_specs=fixed_specs + edge_specs + [strip(4 * cells)],
        out_specs=strip(2 * cells),
        out_shape=jax.ShapeDtypeStruct((total, 2 * cells), F32),
        scratch_shapes=scratch(6 * HALO, 4 * HALO),
        compiler_params=params(),
        name="first_half_rim",
    )(mix, east, north, fwd, bwd, near)

    sizes = dict(lat=lat, levels=levels, tracers=tracers)
    forcing_specs = [
        whole(tiles, height, capacity),
        pl.BlockSpec((total, cells), lambda i: (0, i)),
    ]
    forcing_scratch = [pltpu.VMEM((total, slots), BF16), pltpu.VMEM((8, slots), F32)]
    own_w, own_e = pl.pallas_call(
        functools.partial(forcing_rim_kernel, pairs=pairs, **sizes),
        grid=(2,),
        in_specs=forcing_specs,
        out_specs=[whole(total, cells), whole(total, cells)],
        out_shape=[jax.ShapeDtypeStruct((total, cells), BF16)] * 2,
        scratch_shapes=forcing_scratch,
        compiler_params=params(),
        name="forcing_rim",
    )(got, rim)
    far_w = lax.ppermute(own_e, "tile", ring)
    far_e = lax.ppermute(own_w, "tile", back)
    inner = pl.pallas_call(
        functools.partial(forcing_inner_kernel, **sizes),
        grid=(pairs - 2,),
        in_specs=forcing_specs,
        out_specs=pl.BlockSpec((total, cells), lambda i: (0, i)),
        out_shape=jax.ShapeDtypeStruct((total, inner_width), BF16),
        scratch_shapes=forcing_scratch,
        compiler_params=params(),
        name="forcing_inner",
    )(got, middle)

    out = pl.pallas_call(
        functools.partial(second_half_kernel, lon=lon, levels=levels, total=total),
        grid=(steps,),
        in_specs=fixed_specs
        + edge_specs
        + [strip(cells), strip(cells), strip(inner_width), strip(cells), strip(cells)],
        out_specs=pl.BlockSpec((rows * lon, lat), lambda i: (i, 0)),
        out_shape=jax.ShapeDtypeStruct((total * lon, lat), F32),
        scratch_shapes=scratch(lon + 2 * HALO, lon + 2 * HALO - 2),
        compiler_params=params(),
        name="second_half",
    )(mix, east, north, fwd, bwd, far_w, own_w, inner, own_e, far_e)
    return out.reshape(tracers, levels, lon, lat)


def solution(mesh):
    in_specs = (
        P("ens", None, "tile", None),
        P("ens", "tile", None),
        P("ens", "tile", None),
        P(),
        P("ens", "tile"),
        P("ens", "tile"),
        P("tile", "ens"),
        P("ens", "tile"),
    )
    out_specs = P("ens", None, "tile", None)
    return jax.shard_map(
        per_device, mesh=mesh, in_specs=in_specs, out_specs=out_specs, check_vma=False
    )
```

```python
import functools

import jax
import jax.numpy as jnp
from jax import lax
from jax.experimental import pallas as pl
from jax.experimental.pallas import tpu as pltpu
from jax.sharding import PartitionSpec as P

F32 = jnp.float32
BF16 = jnp.bfloat16
GROUP = 2
HALO = 2
VMEM = 56 * 1024 * 1024


def params(**more):
    return pltpu.CompilerParams(vmem_limit_bytes=VMEM, **more)


def nt_dot(a, b):
    return lax.dot_general(a, b, (((1,), (1,)), ((), ())), preferred_element_type=F32)


def rows16(row):
    return jnp.broadcast_to(row, (16, row.shape[1])).astype(BF16)


def stacked(block, count):
    return jnp.concatenate([block] * count, axis=0)


def pack_kernel(
    kernel_ref, weight_ref, owner_ref, column_ref, out_ref, *, tiles, capacity, lat, pairs
):
    levels, pixels = kernel_ref.shape
    column = column_ref[...]
    longitude = column // lat
    line = lax.broadcasted_iota(jnp.int32, (8, pixels), 0)
    place = jnp.where(
        line == 0,
        (longitude + 1).astype(F32),
        jnp.where(line == 1, (column % lat).astype(F32), 0.0),
    )
    payload = jnp.concatenate(
        [kernel_ref[...].astype(F32), weight_ref[...].astype(F32), place], axis=0
    ).astype(BF16)
    classes = tiles * pairs
    named = owner_ref[...] * pairs + longitude // HALO
    block = min(256, pixels)

    def iota(shape, dim):
        return lax.broadcasted_iota(jnp.int32, shape, dim)

    def flags(mask):
        return mask.astype(F32).astype(BF16)

    upto = flags(iota((block, block), 0) <= iota((block, block), 1))
    carry = jnp.zeros((classes, 1), F32)
    members, counted = [], []
    for start in range(0, pixels, block):
        member = named[:, start : start + block] == iota((classes, block), 0)
        counts = jnp.dot(flags(member), upto, preferred_element_type=F32) + carry
        carry = counts[:, block - 1 : block]
        members.append(member)
        counted.append(counts)
    size = jnp.broadcast_to(carry, (classes, 128))
    row, other = iota((classes, classes), 0), iota((classes, classes), 1)
    same = row // pairs == other // pairs
    sizes = size.astype(BF16)
    before = jnp.dot(flags(same & (other < row)), sizes, preferred_element_type=F32)
    after = jnp.dot(flags(same & (other >= row)), sizes, preferred_element_type=F32)
    pair = iota((classes, 128), 0) % pairs
    slack = pair.astype(F32) * (capacity // pairs) - before
    shift = 1
    while shift < pairs:
        slack = jnp.where(pair >= shift, jnp.maximum(slack, pltpu.roll(slack, shift, 0)), slack)
        shift = 2 * shift
    begin = jnp.minimum(before + slack, capacity - after)[:, :1]
    gather = flags(iota((tiles, classes), 0) == iota((tiles, classes), 1) // pairs)
    ranks = [
        jnp.dot(
            gather,
            jnp.where(member, begin + counts, 0.0).astype(BF16),
            preferred_element_type=F32,
        )
        - 1.0
        for member, counts in zip(members, counted)
    ]
    ranks = jnp.concatenate(ranks, axis=1)
    slot = iota((capacity, pixels), 0).astype(F32).astype(BF16)
    for tile in range(tiles):
        rank = stacked(rows16(ranks[tile : tile + 1, :]), capacity // 16)
        chosen = jnp.where(slot == rank, jnp.ones_like(slot), jnp.zeros_like(slot))
        out_ref[tile] = nt_dot(payload, chosen).astype(BF16)


def both(ref, block, x, lon, levels):
    parts = [
        ref[pl.ds((t * levels + block * 8) * lon + x, 8, stride=lon), :] for t in range(GROUP)
    ]
    return jnp.concatenate(parts, axis=0).astype(BF16)


def edge_kernel(
    field_ref, east_ref, north_ref, level_mix_ref, fwd_ref, bwd_ref, mix_ref, *, lon, levels
):
    step = pl.program_id(0)
    rows = field_ref.shape[0] // lon
    total = rows * pl.num_programs(0)
    for c in range(HALO):
        for block in range(levels // 8):
            spot = c * total + step * rows + block * 8 * GROUP
            at = pl.ds(pl.multiple_of(spot, 16), 8 * GROUP)
            fwd_ref[at, :] = both(field_ref, block, lon - HALO + c, lon, levels)
            bwd_ref[at, :] = both(field_ref, block, c, lon, levels)

    @pl.when(step == 0)
    def _():
        def put(out, place, ref, x):
            spot = HALO * total + place * (levels + 8)
            value = ref[pl.ds(x, levels, stride=lon), :]
            value = jnp.concatenate([value, jnp.zeros((8, value.shape[1]), F32)], axis=0)
            out[spot : spot + levels + 8, :] = value.astype(BF16)

        put(fwd_ref, 0, east_ref, lon - 2)
        put(fwd_ref, 1, east_ref, lon - 1)
        put(fwd_ref, 2, north_ref, lon - 1)
        put(bwd_ref, 0, east_ref, 0)
        put(bwd_ref, 1, north_ref, 0)
        rows = GROUP * levels
        row = lax.broadcasted_iota(jnp.int32, (rows, levels), 0)
        level = row // (8 * GROUP) * 8 + row % 8
        mine = level == lax.broadcasted_iota(jnp.int32, (rows, levels), 1)
        mix = jnp.zeros((rows, rows), F32)
        for t in range(GROUP):
            pick = (mine & (row // 8 % GROUP == t)).astype(F32).astype(BF16)
            mix = mix + nt_dot(nt_dot(pick, level_mix_ref[...]).astype(BF16), pick)
        mix_ref[...] = mix.astype(BF16)


def fill_coefs(east_ref, north_ref, edges, coef_ref, columns, lon, levels, total):
    lat = east_ref.shape[1]
    base = HALO * total

    def far(ref, place):
        spot = base + place * (levels + 8)
        return ref[spot : spot + levels + 8, :].astype(F32)[:levels]

    def own(ref, x):
        return ref[pl.ds(x, levels, stride=lon), :]

    def east(x):
        if x < 0:
            return far(edges[0], x + HALO)
        return own(east_ref, x) if x < lon else far(edges[1], 0)

    def north(x):
        if x < 0:
            return far(edges[0], 2)
        return own(north_ref, x) if x < lon else far(edges[1], 1)

    lane = lax.broadcasted_iota(jnp.int32, (levels, lat), 1)
    for i, x in enumerate(columns):
        at = slice(i * lat, (i + 1) * lat)
        face = jnp.where(lane < lat - 1, north(x), 0.0)
        to_east = jnp.maximum(east(x), 0.0)
        to_west = jnp.minimum(east(x - 1), 0.0)
        to_north = jnp.maximum(face, 0.0)
        to_south = pltpu.roll(jnp.minimum(face, 0.0), 1, 1)
        coef_ref[0, :, at] = (1.0 - to_east) + to_west + (to_south - to_north)
        coef_ref[1, :, at] = to_east
        coef_ref[2, :, at] = -to_west
        coef_ref[3, :, at] = to_north
        coef_ref[4, :, at] = -to_south


def stencil(mixed_ref, coef_ref, start, count, coef_start, lat, levels, emit):
    def column(e):
        return slice(e * lat, (e + 1) * lat)

    for block in range(levels // 8):
        lines = slice(block * 8, block * 8 + 8)
        tracer_rows = [
            slice(block * 8 * GROUP + 8 * t, block * 8 * GROUP + 8 * t + 8) for t in range(GROUP)
        ]
        left = [mixed_ref[r, column(start - 1)] for r in tracer_rows]
        centre = [mixed_ref[r, column(start)] for r in tracer_rows]
        for e in range(start, start + count):
            at = column(coef_start + e - start)
            factor = [coef_ref[j, lines, at] for j in range(5)]
            values = []
            for t, r in enumerate(tracer_rows):
                right = mixed_ref[r, column(e + 1)]
                value = (factor[0] * centre[t] + factor[1] * right) + (
                    factor[2] * left[t] + factor[3] * pltpu.roll(centre[t], lat - 1, 1)
                )
                values.append(value + factor[4] * pltpu.roll(centre[t], 1, 1))
                left[t], centre[t] = centre[t], right
            emit(block, e, values)


def two_steps(mix_ref, field_ref, mixed_ref, coef_ref, start, count, coef_start, lat, levels, put):
    def mix(lo, hi):
        for e in range(lo, hi, 2):
            at = slice(e * lat, (e + 2) * lat)
            mixed_ref[:, at] = jnp.dot(mix_ref[...], field_ref[:, at], preferred_element_type=F32)

    def keep(block, e, values):
        at = slice(block * 8 * GROUP, (block + 1) * 8 * GROUP)
        field_ref[at, e * lat : (e + 1) * lat] = jnp.concatenate(values, axis=0).astype(BF16)

    mix(start, start + count)
    stencil(mixed_ref, coef_ref, start + 1, count - 2, coef_start, lat, levels, keep)
    mix(start + 1, start + count - 1)
    stencil(mixed_ref, coef_ref, start + 2, count - 4, coef_start + 1, lat, levels, put)


def inner_kernel(
    mix_ref, east_ref, north_ref, in_ref, out_ref, near_ref, coef_ref, field_ref, mixed_ref,
    *, lon, levels,
):
    lat = in_ref.shape[1]

    @pl.when(pl.program_id(0) == 0)
    def _():
        fill_coefs(east_ref, north_ref, None, coef_ref, range(1, lon - 1), lon, levels, 0)

    for x in range(lon):
        for block in range(levels // 8):
            at = slice(block * 8 * GROUP, (block + 1) * 8 * GROUP)
            field_ref[at, x * lat : (x + 1) * lat] = both(in_ref, block, x, lon, levels)
    side = 2 * HALO * lat
    near_ref[:, :side] = field_ref[:, :side]
    near_ref[:, side:] = field_ref[:, lon * lat - side :]

    def put(block, e, values):
        for t, value in enumerate(values):
            row = block * 8 * GROUP + 8 * t
            out_ref[row : row + 8, (e - HALO) * lat : (e - HALO + 1) * lat] = value

    two_steps(mix_ref, field_ref, mixed_ref, coef_ref, 0, lon, 0, lat, levels, put)


def rim_kernel(
    mix_ref, east_ref, north_ref, fwd_ref, bwd_ref, near_ref, out_ref, coef_ref, field_ref,
    mixed_ref, *, lon, levels, total,
):
    step = pl.program_id(0)
    lat = fwd_ref.shape[1]
    rows = near_ref.shape[0]
    wide = 3 * HALO

    @pl.when(step == 0)
    def _():
        columns = list(range(1 - HALO, HALO + 1)) + list(range(lon - HALO - 1, lon + HALO - 1))
        fill_coefs(
            east_ref, north_ref, (fwd_ref, bwd_ref), coef_ref, columns, lon, levels, total
        )

    for c in range(HALO):
        at = pl.ds(pl.multiple_of(c * total + step * rows, 16), rows)
        field_ref[:, c * lat : (c + 1) * lat] = fwd_ref[at, :]
        e = wide + 2 * HALO + c
        field_ref[:, e * lat : (e + 1) * lat] = bwd_ref[at, :]
    side = 2 * HALO * lat
    field_ref[:, HALO * lat : HALO * lat + side] = near_ref[:, :side]
    field_ref[:, wide * lat : wide * lat + side] = near_ref[:, side:]
    for half in range(2):
        start = half * wide

        def put(block, e, values):
            spot = (e - start - HALO + half * HALO) * lat
            for t, value in enumerate(values):
                row = block * 8 * GROUP + 8 * t
                out_ref[row : row + 8, spot : spot + lat] = value

        two_steps(
            mix_ref, field_ref, mixed_ref, coef_ref, start, wide, half * 2 * HALO, lat, levels, put
        )


def second_half_kernel(
    mix_ref, east_ref, north_ref, fwd_ref, bwd_ref, far_w_ref, own_w_ref, inner_ref, own_e_ref,
    far_e_ref, out_ref, coef_ref, field_ref, mixed_ref, *, lon, levels, total,
):
    lat = out_ref.shape[1]

    @pl.when(pl.program_id(0) == 0)
    def _():
        columns = range(1 - HALO, lon + HALO - 1)
        fill_coefs(
            east_ref, north_ref, (fwd_ref, bwd_ref), coef_ref, columns, lon, levels, total
        )

    spot = 0
    for ref in (far_w_ref, own_w_ref, inner_ref, own_e_ref, far_e_ref):
        width = ref.shape[-1]
        field_ref[:, spot : spot + width] = ref[...]
        spot = spot + width

    def put(block, e, values):
        for t, value in enumerate(values):
            first = (t * levels + block * 8) * lon + e - HALO
            out_ref[pl.ds(first, 8, stride=lon), :] = value

    two_steps(
        mix_ref, field_ref, mixed_ref, coef_ref, 0, lon + 2 * HALO, 0, lat, levels, put
    )


def regions_of(capacity):
    return capacity // 64 if capacity % 128 == 0 else 1


def regroup(got_ref, store):
    tiles, height, capacity = got_ref.shape
    if regions_of(capacity) == 1:
        for tile in range(tiles):
            store(tile * capacity, got_ref[tile].astype(F32))
        return
    low = lax.broadcasted_iota(jnp.int32, (height, 128), 1) < 64
    for tile in range(0, tiles, 2):
        for half in range(capacity // 128):
            at = slice(half * 128, half * 128 + 128)
            one, two = got_ref[tile, :, at].astype(F32), got_ref[tile + 1, :, at].astype(F32)
            spot = 2 * half * tiles * 64 + tile * 64
            store(spot, jnp.where(low, one, pltpu.roll(two, 64, 1)))
            store(spot + tiles * 64, jnp.where(low, pltpu.roll(one, 64, 1), two))


def forcing(
    got_ref, field_ref, weighted_ref, place_ref, range_ref, total_ref, step, pair,
    *, lat, levels, tracers,
):
    tiles, _, capacity = got_ref.shape
    cells = HALO * lat
    parts = regions_of(capacity)
    wide = tiles * capacity // parts

    @pl.when(step == 0)
    def _():
        def store(spot, got):
            at = slice(spot, spot + got.shape[1])
            row = 0
            for t in range(0, tracers, GROUP):
                for block in range(0, levels, 8):
                    kernel = got[block : block + 8]
                    pieces = [
                        kernel * got[levels + j : levels + j + 1, :] for j in range(t, t + GROUP)
                    ]
                    value = jnp.concatenate(pieces, axis=0).astype(BF16)
                    weighted_ref[row : row + 8 * GROUP, at] = value
                    row = row + 8 * GROUP
            first = levels + tracers
            column = (got[first : first + 1, :] - 1.0) * lat + got[first + 1 : first + 2, :]
            place_ref[:, at] = jnp.broadcast_to(column, (8, got.shape[1]))

        regroup(got_ref, store)
        for part in range(parts):
            place = place_ref[:, part * wide : (part + 1) * wide]
            far = 1e6
            range_ref[2 * part] = jnp.min(jnp.where(place < 0.0, far, place))
            range_ref[2 * part + 1] = jnp.max(place)

    total_ref[...] = field_ref[...]
    offset = (pair * cells).astype(F32)
    for part in range(parts):
        held = (range_ref[2 * part] < offset + cells) & (range_ref[2 * part + 1] >= offset)

        @pl.when(held)
        def _():
            at = slice(part * wide, (part + 1) * wide)
            key = rows16(place_ref[0:1, at] - offset)
            cell = lax.broadcasted_iota(jnp.int32, (cells, wide), 0).astype(F32).astype(BF16)
            hit = cell == stacked(key, cells // 16)
            one_hot = jnp.where(hit, jnp.ones_like(cell), jnp.zeros_like(cell))
            total_ref[...] += nt_dot(weighted_ref[:, at], one_hot)

    return total_ref[...].astype(BF16)


def forcing_inner_kernel(got_ref, field_ref, out_ref, *scratch, **sizes):
    step = pl.program_id(0)
    out_ref[...] = forcing(got_ref, field_ref, *scratch, step, step + 1, **sizes)


def forcing_rim_kernel(got_ref, field_ref, west_ref, east_ref, *scratch, pairs, **sizes):
    step = pl.program_id(0)
    value = forcing(got_ref, field_ref, *scratch, step, step * (pairs - 1), **sizes)

    @pl.when(step == 0)
    def _():
        west_ref[...] = value

    @pl.when(step == 1)
    def _():
        east_ref[...] = value


def per_device(
    adjoint_in,
    east_courant,
    north_courant,
    level_mix,
    avg_kernel,
    pixel_weight,
    pixel_owner,
    pixel_column,
):
    tracers, levels, lon, lat = adjoint_in.shape
    pixels = avg_kernel.shape[1]
    tiles = lax.axis_size("tile")
    capacity = 4 * pixels // tiles
    slots = tiles * capacity
    total = tracers * levels
    steps = tracers // GROUP
    rows = GROUP * levels
    ring = [(i, (i + 1) % tiles) for i in range(tiles)]
    back = [((i + 1) % tiles, i) for i in range(tiles)]

    field = adjoint_in.reshape(total * lon, lat)
    east = east_courant.reshape(levels * lon, lat)
    north = north_courant.reshape(levels * lon, lat)
    pairs = lon // HALO
    height = levels + tracers + 8
    payload = pl.pallas_call(
        functools.partial(pack_kernel, tiles=tiles, capacity=capacity, lat=lat, pairs=pairs),
        out_shape=jax.ShapeDtypeStruct((tiles, height, capacity), BF16),
        compiler_params=params(),
        name="pack",
    )(avg_kernel, pixel_weight, pixel_owner.reshape(1, pixels), pixel_column)
    got = lax.all_to_all(payload, "tile", split_axis=0, concat_axis=0, tiled=True)

    fwd_rows = HALO * total + 3 * (levels + 8)
    bwd_rows = HALO * total + 2 * (levels + 8)
    whole = lambda *shape: pl.BlockSpec(shape, lambda i: (0,) * len(shape))
    fwd, bwd, mix = pl.pallas_call(
        functools.partial(edge_kernel, lon=lon, levels=levels),
        grid=(steps,),
        in_specs=[
            pl.BlockSpec((rows * lon, lat), lambda i: (i, 0)),
            whole(levels * lon, lat),
            whole(levels * lon, lat),
            whole(levels, levels),
        ],
        out_specs=[whole(fwd_rows, lat), whole(bwd_rows, lat), whole(rows, rows)],
        out_shape=[
            jax.ShapeDtypeStruct((fwd_rows, lat), BF16),
            jax.ShapeDtypeStruct((bwd_rows, lat), BF16),
            jax.ShapeDtypeStruct((rows, rows), BF16),
        ],
        compiler_params=params(),
        name="edges",
    )(field, east, north, level_mix)
    fwd = lax.ppermute(fwd, "tile", ring)
    bwd = lax.ppermute(bwd, "tile", back)

    def scratch(columns, coefs):
        return [
            pltpu.VMEM((5, levels, coefs * lat), F32),
            pltpu.VMEM((rows, columns * lat), BF16),
            pltpu.VMEM((rows, columns * lat), F32),
        ]

    strip = lambda width: pl.BlockSpec((rows, width), lambda i: (i, 0))
    cells = HALO * lat
    fixed_specs = [whole(rows, rows), whole(levels * lon, lat), whole(levels * lon, lat)]
    edge_specs = [whole(fwd_rows, lat), whole(bwd_rows, lat)]
    inner_width = (lon - 2 * HALO) * lat
    middle, near = pl.pallas_call(
        functools.partial(inner_kernel, lon=lon, levels=levels),
        grid=(steps,),
        in_specs=fixed_specs + [pl.BlockSpec((rows * lon, lat), lambda i: (i, 0))],
        out_specs=[strip(inner_width), strip(4 * cells)],
        out_shape=[
            jax.ShapeDtypeStruct((total, inner_width), F32),
            jax.ShapeDtypeStruct((total, 4 * cells), BF16),
        ],
        scratch_shapes=scratch(lon, lon - 2),
        compiler_params=params(),
        name="first_half_inner",
    )(mix, east, north, field)
    rim = pl.pallas_call(
        functools.partial(rim_kernel, lon=lon, levels=levels, total=total),
        grid=(steps,),
        in_specs=fixed_specs + edge_specs + [strip(4 * cells)],
        out_specs=strip(2 * cells),
        out_shape=jax.ShapeDtypeStruct((total, 2 * cells), F32),
        scratch_shapes=scratch(6 * HALO, 4 * HALO),
        compiler_params=params(),
        name="first_half_rim",
    )(mix, east, north, fwd, bwd, near)

    sizes = dict(lat=lat, levels=levels, tracers=tracers)
    forcing_specs = [
        whole(tiles, height, capacity),
        pl.BlockSpec((total, cells), lambda i: (0, i)),
    ]
    forcing_scratch = [
        pltpu.VMEM((total, slots), BF16),
        pltpu.VMEM((8, slots), F32),
        pltpu.SMEM((2 * regions_of(capacity),), F32),
        pltpu.VMEM((total, cells), F32),
    ]
    own_w, own_e = pl.pallas_call(
        functools.partial(forcing_rim_kernel, pairs=pairs, **sizes),
        grid=(2,),
        in_specs=forcing_specs,
        out_specs=[whole(total, cells), whole(total, cells)],
        out_shape=[jax.ShapeDtypeStruct((total, cells), BF16)] * 2,
        scratch_shapes=forcing_scratch,
        compiler_params=params(),
        name="forcing_rim",
    )(got, rim)
    far_w = lax.ppermute(own_e, "tile", ring)
    far_e = lax.ppermute(own_w, "tile", back)
    inner = pl.pallas_call(
        functools.partial(forcing_inner_kernel, **sizes),
        grid=(pairs - 2,),
        in_specs=forcing_specs,
        out_specs=pl.BlockSpec((total, cells), lambda i: (0, i)),
        out_shape=jax.ShapeDtypeStruct((total, inner_width), BF16),
        scratch_shapes=forcing_scratch,
        compiler_params=params(),
        name="forcing_inner",
    )(got, middle)

    out = pl.pallas_call(
        functools.partial(second_half_kernel, lon=lon, levels=levels, total=total),
        grid=(steps,),
        in_specs=fixed_specs
        + edge_specs
        + [strip(cells), strip(cells), strip(inner_width), strip(cells), strip(cells)],
        out_specs=pl.BlockSpec((rows * lon, lat), lambda i: (i, 0)),
        out_shape=jax.ShapeDtypeStruct((total * lon, lat), F32),
        scratch_shapes=scratch(lon + 2 * HALO, lon + 2 * HALO - 2),
        compiler_params=params(),
        name="second_half",
    )(mix, east, north, fwd, bwd, far_w, own_w, inner, own_e, far_e)
    return out.reshape(tracers, levels, lon, lat)


def solution(mesh):
    in_specs = (
        P("ens", None, "tile", None),
        P("ens", "tile", None),
        P("ens", "tile", None),
        P(),
        P("ens", "tile"),
        P("ens", "tile"),
        P("tile", "ens"),
        P("ens", "tile"),
    )
    out_specs = P("ens", None, "tile", None)
    return jax.shard_map(
        per_device, mesh=mesh, in_specs=in_specs, out_specs=out_specs, check_vma=False
    )
```

```python
import functools

import jax
import jax.numpy as jnp
from jax import lax
from jax.experimental import pallas as pl
from jax.experimental.pallas import tpu as pltpu
from jax.sharding import PartitionSpec as P

F32 = jnp.float32
BF16 = jnp.bfloat16
GROUP = 2
HALO = 2
VMEM = 56 * 1024 * 1024


def params(**more):
    return pltpu.CompilerParams(vmem_limit_bytes=VMEM, **more)


def nt_dot(a, b):
    return lax.dot_general(a, b, (((1,), (1,)), ((), ())), preferred_element_type=F32)


def rows16(row):
    return jnp.broadcast_to(row, (16, row.shape[1])).astype(BF16)


def stacked(block, count):
    return jnp.concatenate([block] * count, axis=0)


def pack_kernel(
    kernel_ref, weight_ref, owner_ref, column_ref, out_ref, *, tiles, capacity, lat, pairs
):
    levels, pixels = kernel_ref.shape
    column = column_ref[...]
    longitude = column // lat
    line = lax.broadcasted_iota(jnp.int32, (8, pixels), 0)
    place = jnp.where(
        line == 0,
        (longitude + 1).astype(F32),
        jnp.where(line == 1, (column % lat).astype(F32), 0.0),
    )
    payload = jnp.concatenate(
        [kernel_ref[...].astype(F32), weight_ref[...].astype(F32), place], axis=0
    ).astype(BF16)
    classes = tiles * pairs
    named = owner_ref[...] * pairs + longitude // HALO
    block = min(256, pixels)

    def iota(shape, dim):
        return lax.broadcasted_iota(jnp.int32, shape, dim)

    def flags(mask):
        return mask.astype(F32).astype(BF16)

    upto = flags(iota((block, block), 0) <= iota((block, block), 1))
    carry = jnp.zeros((classes, 1), F32)
    members, counted = [], []
    for start in range(0, pixels, block):
        member = named[:, start : start + block] == iota((classes, block), 0)
        counts = jnp.dot(flags(member), upto, preferred_element_type=F32) + carry
        carry = counts[:, block - 1 : block]
        members.append(member)
        counted.append(counts)
    size = jnp.broadcast_to(carry, (classes, 128))
    row, other = iota((classes, classes), 0), iota((classes, classes), 1)
    same = row // pairs == other // pairs
    sizes = size.astype(BF16)
    before = jnp.dot(flags(same & (other < row)), sizes, preferred_element_type=F32)
    after = jnp.dot(flags(same & (other >= row)), sizes, preferred_element_type=F32)
    pair = iota((classes, 128), 0) % pairs
    slack = pair.astype(F32) * (capacity // pairs) - before
    shift = 1
    while shift < pairs:
        slack = jnp.where(pair >= shift, jnp.maximum(slack, pltpu.roll(slack, shift, 0)), slack)
        shift = 2 * shift
    begin = jnp.minimum(before + slack, capacity - after)[:, :1]
    gather = flags(iota((tiles, classes), 0) == iota((tiles, classes), 1) // pairs)
    ranks = [
        jnp.dot(
            gather,
            jnp.where(member, begin + counts, 0.0).astype(BF16),
            preferred_element_type=F32,
        )
        - 1.0
        for member, counts in zip(members, counted)
    ]
    ranks = jnp.concatenate(ranks, axis=1)
    slot = iota((capacity, pixels), 0).astype(F32).astype(BF16)
    for tile in range(tiles):
        rank = stacked(rows16(ranks[tile : tile + 1, :]), capacity // 16)
        chosen = jnp.where(slot == rank, jnp.ones_like(slot), jnp.zeros_like(slot))
        out_ref[tile] = nt_dot(payload, chosen).astype(BF16)


def both(ref, block, x, lon, levels):
    parts = [
        ref[pl.ds((t * levels + block * 8) * lon + x, 8, stride=lon), :] for t in range(GROUP)
    ]
    return jnp.concatenate(parts, axis=0).astype(BF16)


def edge_kernel(
    field_ref, east_ref, north_ref, level_mix_ref, fwd_ref, bwd_ref, mix_ref, *, lon, levels
):
    step = pl.program_id(0)
    rows = GROUP * levels
    groups = field_ref.shape[0] // (rows * lon)
    total = rows * groups * pl.num_programs(0)
    for group in range(groups):
        view = field_ref.at[group * rows * lon : (group + 1) * rows * lon, :]
        for c in range(HALO):
            for block in range(levels // 8):
                spot = c * total + (step * groups + group) * rows + block * 8 * GROUP
                at = pl.ds(pl.multiple_of(spot, 16), 8 * GROUP)
                fwd_ref[at, :] = both(view, block, lon - HALO + c, lon, levels)
                bwd_ref[at, :] = both(view, block, c, lon, levels)

    @pl.when(step == 0)
    def _():
        def put(out, place, ref, x):
            spot = HALO * total + place * (levels + 8)
            value = ref[pl.ds(x, levels, stride=lon), :]
            value = jnp.concatenate([value, jnp.zeros((8, value.shape[1]), F32)], axis=0)
            out[spot : spot + levels + 8, :] = value.astype(BF16)

        put(fwd_ref, 0, east_ref, lon - 2)
        put(fwd_ref, 1, east_ref, lon - 1)
        put(fwd_ref, 2, north_ref, lon - 1)
        put(bwd_ref, 0, east_ref, 0)
        put(bwd_ref, 1, north_ref, 0)
        rows = GROUP * levels
        row = lax.broadcasted_iota(jnp.int32, (rows, levels), 0)
        level = row // (8 * GROUP) * 8 + row % 8
        mine = level == lax.broadcasted_iota(jnp.int32, (rows, levels), 1)
        mix = jnp.zeros((rows, rows), F32)
        for t in range(GROUP):
            pick = (mine & (row // 8 % GROUP == t)).astype(F32).astype(BF16)
            mix = mix + nt_dot(nt_dot(pick, level_mix_ref[...]).astype(BF16), pick)
        mix_ref[...] = mix.astype(BF16)


def fill_coefs(east_ref, north_ref, edges, coef_ref, columns, lon, levels, total):
    lat = east_ref.shape[1]
    base = HALO * total

    def far(ref, place):
        spot = base + place * (levels + 8)
        return ref[spot : spot + levels + 8, :].astype(F32)[:levels]

    def own(ref, x):
        return ref[pl.ds(x, levels, stride=lon), :]

    def east(x):
        if x < 0:
            return far(edges[0], x + HALO)
        return own(east_ref, x) if x < lon else far(edges[1], 0)

    def north(x):
        if x < 0:
            return far(edges[0], 2)
        return own(north_ref, x) if x < lon else far(edges[1], 1)

    lane = lax.broadcasted_iota(jnp.int32, (levels, lat), 1)
    for i, x in enumerate(columns):
        at = slice(i * lat, (i + 1) * lat)
        face = jnp.where(lane < lat - 1, north(x), 0.0)
        to_east = jnp.maximum(east(x), 0.0)
        to_west = jnp.minimum(east(x - 1), 0.0)
        to_north = jnp.maximum(face, 0.0)
        to_south = pltpu.roll(jnp.minimum(face, 0.0), 1, 1)
        coef_ref[0, :, at] = (1.0 - to_east) + to_west + (to_south - to_north)
        coef_ref[1, :, at] = to_east
        coef_ref[2, :, at] = -to_west
        coef_ref[3, :, at] = to_north
        coef_ref[4, :, at] = -to_south


def stencil(mixed_ref, coef_ref, start, count, coef_start, lat, levels, emit):
    def column(e):
        return slice(e * lat, (e + 1) * lat)

    for block in range(levels // 8):
        lines = slice(block * 8, block * 8 + 8)
        tracer_rows = [
            slice(block * 8 * GROUP + 8 * t, block * 8 * GROUP + 8 * t + 8) for t in range(GROUP)
        ]
        left = [mixed_ref[r, column(start - 1)] for r in tracer_rows]
        centre = [mixed_ref[r, column(start)] for r in tracer_rows]
        for e in range(start, start + count):
            at = column(coef_start + e - start)
            factor = [coef_ref[j, lines, at] for j in range(5)]
            values = []
            for t, r in enumerate(tracer_rows):
                right = mixed_ref[r, column(e + 1)]
                value = (factor[0] * centre[t] + factor[1] * right) + (
                    factor[2] * left[t] + factor[3] * pltpu.roll(centre[t], lat - 1, 1)
                )
                values.append(value + factor[4] * pltpu.roll(centre[t], 1, 1))
                left[t], centre[t] = centre[t], right
            emit(block, e, values)


def two_steps(mix_ref, field_ref, mixed_ref, coef_ref, start, count, coef_start, lat, levels, put):
    def mix(lo, hi):
        for e in range(lo, hi, 2):
            at = slice(e * lat, (e + 2) * lat)
            mixed_ref[:, at] = jnp.dot(mix_ref[...], field_ref[:, at], preferred_element_type=F32)

    def keep(block, e, values):
        at = slice(block * 8 * GROUP, (block + 1) * 8 * GROUP)
        field_ref[at, e * lat : (e + 1) * lat] = jnp.concatenate(values, axis=0).astype(BF16)

    mix(start, start + count)
    stencil(mixed_ref, coef_ref, start + 1, count - 2, coef_start, lat, levels, keep)
    mix(start + 1, start + count - 1)
    stencil(mixed_ref, coef_ref, start + 2, count - 4, coef_start + 1, lat, levels, put)


def inner_kernel(
    mix_ref, east_ref, north_ref, in_ref, out_ref, near_ref, coef_ref, field_ref, mixed_ref,
    *, lon, levels,
):
    lat = in_ref.shape[1]

    @pl.when(pl.program_id(0) == 0)
    def _():
        fill_coefs(east_ref, north_ref, None, coef_ref, range(1, lon - 1), lon, levels, 0)

    for x in range(lon):
        for block in range(levels // 8):
            at = slice(block * 8 * GROUP, (block + 1) * 8 * GROUP)
            field_ref[at, x * lat : (x + 1) * lat] = both(in_ref, block, x, lon, levels)
    side = 2 * HALO * lat
    near_ref[:, :side] = field_ref[:, :side]
    near_ref[:, side:] = field_ref[:, lon * lat - side :]

    def put(block, e, values):
        for t, value in enumerate(values):
            row = block * 8 * GROUP + 8 * t
            out_ref[row : row + 8, (e - HALO) * lat : (e - HALO + 1) * lat] = value

    two_steps(mix_ref, field_ref, mixed_ref, coef_ref, 0, lon, 0, lat, levels, put)


def rim_kernel(
    mix_ref, east_ref, north_ref, fwd_ref, bwd_ref, near_ref, got_ref, west_out_ref, east_out_ref,
    coef_ref, field_ref, mixed_ref, weighted_ref, place_ref, range_ref, total_ref,
    *, lon, levels, tracers,
):
    total = near_ref.shape[0]
    lat = fwd_ref.shape[1]
    rows = GROUP * levels
    wide = 3 * HALO
    columns = list(range(1 - HALO, HALO + 1)) + list(range(lon - HALO - 1, lon + HALO - 1))
    fill_coefs(east_ref, north_ref, (fwd_ref, bwd_ref), coef_ref, columns, lon, levels, total)

    def group_of(group, carry):
        for c in range(HALO):
            at = pl.ds(pl.multiple_of(c * total + group * rows, 16), rows)
            field_ref[:, c * lat : (c + 1) * lat] = fwd_ref[at, :]
            e = wide + 2 * HALO + c
            field_ref[:, e * lat : (e + 1) * lat] = bwd_ref[at, :]
        side = 2 * HALO * lat
        mine = pl.ds(pl.multiple_of(group * rows, 16), rows)
        field_ref[:, HALO * lat : HALO * lat + side] = near_ref[mine, :side]
        field_ref[:, wide * lat : wide * lat + side] = near_ref[mine, side:]
        for half in range(2):
            start = half * wide

            def put(block, e, values):
                spot = (e - start - HALO + half * HALO) * lat
                for t, value in enumerate(values):
                    row = pl.multiple_of(group * rows + block * 8 * GROUP + 8 * t, 8)
                    total_ref[pl.ds(row, 8), spot : spot + lat] = value

            two_steps(
                mix_ref, field_ref, mixed_ref, coef_ref, start, wide, half * 2 * HALO, lat,
                levels, put,
            )
        return carry

    lax.fori_loop(0, total // rows, group_of, 0)
    weigh(got_ref, weighted_ref, place_ref, range_ref, lat, levels, tracers)
    cells = HALO * lat
    for side, out_ref in ((0, west_out_ref), (1, east_out_ref)):
        at = slice(side * cells, (side + 1) * cells)
        pair = side * (lon // HALO - 1)
        add_forcing(weighted_ref, place_ref, range_ref, total_ref, at, float(pair * cells))
        out_ref[...] = total_ref[:, at].astype(BF16)


def second_half_kernel(
    mix_ref, east_hbm, north_hbm, fwd_hbm, bwd_hbm, far_w_hbm, own_w_hbm, inner_hbm, own_e_hbm,
    far_e_hbm, out_hbm, east_ref, north_ref, fwd_ref, bwd_ref, coef_ref, field_ref, mixed_ref,
    result_ref, side_sems, field_sems, out_sems, *, lon, levels, total,
):
    lat = out_hbm.shape[1]
    rows = GROUP * levels
    groups = total // rows
    sides = [
        pltpu.make_async_copy(source, target, side_sems.at[i])
        for i, (source, target) in enumerate(
            (
                (east_hbm, east_ref),
                (north_hbm, north_ref),
                (fwd_hbm, fwd_ref),
                (bwd_hbm, bwd_ref),
            )
        )
    ]

    def pieces(group):
        at = pl.ds(pl.multiple_of(group * rows, 16), rows)
        copies, spot = [], 0
        for i, ref in enumerate((far_w_hbm, own_w_hbm, inner_hbm, own_e_hbm, far_e_hbm)):
            width = ref.shape[1]
            target = field_ref.at[at, pl.ds(spot, width)]
            copies.append(pltpu.make_async_copy(ref.at[at, :], target, field_sems.at[group, i]))
            spot = spot + width
        return copies

    def leave(group):
        at = pl.ds(pl.multiple_of(group * rows * lon, 16), rows * lon)
        return pltpu.make_async_copy(result_ref.at[at, :], out_hbm.at[at, :], out_sems.at[group])

    for copy in sides:
        copy.start()
    for group in range(groups):
        for copy in pieces(group):
            copy.start()
    for copy in sides:
        copy.wait()
    columns = range(1 - HALO, lon + HALO - 1)
    fill_coefs(east_ref, north_ref, (fwd_ref, bwd_ref), coef_ref, columns, lon, levels, total)

    def group_of(group, carry):
        for copy in pieces(group):
            copy.wait()
        view = field_ref.at[pl.ds(pl.multiple_of(group * rows, 16), rows), :]
        base = pl.multiple_of(group * rows * lon, 16)
        result = result_ref.at[pl.ds(base, rows * lon), :]

        def put(block, e, values):
            for t, value in enumerate(values):
                first = (t * levels + block * 8) * lon + e - HALO
                result[pl.ds(first, 8, stride=lon), :] = value

        two_steps(
            mix_ref, view, mixed_ref, coef_ref, 0, lon + 2 * HALO, 0, lat, levels, put
        )
        leave(group).start()
        return carry

    lax.fori_loop(0, groups, group_of, 0)
    for group in range(groups):
        leave(group).wait()


def regions_of(capacity):
    return capacity // 64 if capacity % 128 == 0 else 1


def regroup(got_ref, store):
    tiles, height, capacity = got_ref.shape
    if regions_of(capacity) == 1:
        for tile in range(tiles):
            store(tile * capacity, got_ref[tile].astype(F32))
        return
    low = lax.broadcasted_iota(jnp.int32, (height, 128), 1) < 64
    for tile in range(0, tiles, 2):
        for half in range(capacity // 128):
            at = slice(half * 128, half * 128 + 128)
            one, two = got_ref[tile, :, at].astype(F32), got_ref[tile + 1, :, at].astype(F32)
            spot = 2 * half * tiles * 64 + tile * 64
            store(spot, jnp.where(low, one, pltpu.roll(two, 64, 1)))
            store(spot + tiles * 64, jnp.where(low, pltpu.roll(one, 64, 1), two))


def weigh(got_ref, weighted_ref, place_ref, range_ref, lat, levels, tracers):
    tiles, _, capacity = got_ref.shape
    parts = regions_of(capacity)
    wide = tiles * capacity // parts

    def store(spot, got):
        at = slice(spot, spot + got.shape[1])
        row = 0
        for t in range(0, tracers, GROUP):
            for block in range(0, levels, 8):
                kernel = got[block : block + 8]
                pieces = [
                    kernel * got[levels + j : levels + j + 1, :] for j in range(t, t + GROUP)
                ]
                value = jnp.concatenate(pieces, axis=0).astype(BF16)
                weighted_ref[row : row + 8 * GROUP, at] = value
                row = row + 8 * GROUP
        first = levels + tracers
        column = (got[first : first + 1, :] - 1.0) * lat + got[first + 1 : first + 2, :]
        place_ref[:, at] = jnp.broadcast_to(column, (8, got.shape[1]))

    regroup(got_ref, store)
    for part in range(parts):
        place = place_ref[:, part * wide : (part + 1) * wide]
        range_ref[2 * part] = jnp.min(jnp.where(place < 0.0, 1e6, place))
        range_ref[2 * part + 1] = jnp.max(place)


def add_forcing(weighted_ref, place_ref, range_ref, total_ref, columns, offset):
    cells = total_ref[:, columns].shape[1]
    parts = range_ref.shape[0] // 2
    wide = weighted_ref.shape[1] // parts
    for part in range(parts):
        held = (range_ref[2 * part] < offset + cells) & (range_ref[2 * part + 1] >= offset)

        @pl.when(held)
        def _():
            at = slice(part * wide, (part + 1) * wide)
            key = rows16(place_ref[0:1, at] - offset)
            cell = lax.broadcasted_iota(jnp.int32, (cells, wide), 0).astype(F32).astype(BF16)
            hit = cell == stacked(key, cells // 16)
            one_hot = jnp.where(hit, jnp.ones_like(cell), jnp.zeros_like(cell))
            total_ref[:, columns] += nt_dot(weighted_ref[:, at], one_hot)


def forcing_inner_kernel(
    got_ref, field_hbm, out_hbm, weighted_ref, place_ref, range_ref, total_ref, rounded_ref,
    in_sems, out_sems, *, lat, levels, tracers,
):
    cells = HALO * lat
    count = field_hbm.shape[1] // cells

    def at(i):
        return pl.ds(pl.multiple_of(i * cells, cells), cells)

    def enter(i):
        return pltpu.make_async_copy(
            field_hbm.at[:, at(i)], total_ref.at[:, at(i)], in_sems.at[i]
        )

    def leave(i):
        return pltpu.make_async_copy(
            rounded_ref.at[:, at(i)], out_hbm.at[:, at(i)], out_sems.at[i]
        )

    for i in range(count):
        enter(i).start()
    weigh(got_ref, weighted_ref, place_ref, range_ref, lat, levels, tracers)

    def pair_of(i, carry):
        enter(i).wait()
        offset = ((i + 1) * cells).astype(F32)
        add_forcing(weighted_ref, place_ref, range_ref, total_ref, at(i), offset)
        rounded_ref[:, at(i)] = total_ref[:, at(i)].astype(BF16)
        leave(i).start()
        return carry

    lax.fori_loop(0, count, pair_of, 0)
    for i in range(count):
        leave(i).wait()


def per_device(
    adjoint_in,
    east_courant,
    north_courant,
    level_mix,
    avg_kernel,
    pixel_weight,
    pixel_owner,
    pixel_column,
):
    tracers, levels, lon, lat = adjoint_in.shape
    pixels = avg_kernel.shape[1]
    tiles = lax.axis_size("tile")
    capacity = 4 * pixels // tiles
    slots = tiles * capacity
    total = tracers * levels
    steps = tracers // GROUP
    rows = GROUP * levels
    ring = [(i, (i + 1) % tiles) for i in range(tiles)]
    back = [((i + 1) % tiles, i) for i in range(tiles)]

    field = adjoint_in.reshape(total * lon, lat)
    east = east_courant.reshape(levels * lon, lat)
    north = north_courant.reshape(levels * lon, lat)
    pairs = lon // HALO
    height = levels + tracers + 8
    payload = pl.pallas_call(
        functools.partial(pack_kernel, tiles=tiles, capacity=capacity, lat=lat, pairs=pairs),
        out_shape=jax.ShapeDtypeStruct((tiles, height, capacity), BF16),
        compiler_params=params(),
        name="pack",
    )(avg_kernel, pixel_weight, pixel_owner.reshape(1, pixels), pixel_column)
    got = lax.all_to_all(payload, "tile", split_axis=0, concat_axis=0, tiled=True)

    fwd_rows = HALO * total + 3 * (levels + 8)
    bwd_rows = HALO * total + 2 * (levels + 8)
    whole = lambda *shape: pl.BlockSpec(shape, lambda i: (0,) * len(shape))
    fwd, bwd, mix = pl.pallas_call(
        functools.partial(edge_kernel, lon=lon, levels=levels),
        grid=(2,),
        in_specs=[
            pl.BlockSpec((total * lon // 2, lat), lambda i: (i, 0)),
            whole(levels * lon, lat),
            whole(levels * lon, lat),
            whole(levels, levels),
        ],
        out_specs=[whole(fwd_rows, lat), whole(bwd_rows, lat), whole(rows, rows)],
        out_shape=[
            jax.ShapeDtypeStruct((fwd_rows, lat), BF16),
            jax.ShapeDtypeStruct((bwd_rows, lat), BF16),
            jax.ShapeDtypeStruct((rows, rows), BF16),
        ],
        compiler_params=params(),
        name="edges",
    )(field, east, north, level_mix)
    fwd = lax.ppermute(fwd, "tile", ring)
    bwd = lax.ppermute(bwd, "tile", back)

    def scratch(columns, coefs):
        return [
            pltpu.VMEM((5, levels, coefs * lat), F32),
            pltpu.VMEM((rows, columns * lat), BF16),
            pltpu.VMEM((rows, columns * lat), F32),
        ]

    strip = lambda width: pl.BlockSpec((rows, width), lambda i: (i, 0))
    cells = HALO * lat
    fixed_specs = [whole(rows, rows), whole(levels * lon, lat), whole(levels * lon, lat)]
    inner_width = (lon - 2 * HALO) * lat
    middle, near = pl.pallas_call(
        functools.partial(inner_kernel, lon=lon, levels=levels),
        grid=(steps,),
        in_specs=fixed_specs + [pl.BlockSpec((rows * lon, lat), lambda i: (i, 0))],
        out_specs=[strip(inner_width), strip(4 * cells)],
        out_shape=[
            jax.ShapeDtypeStruct((total, inner_width), F32),
            jax.ShapeDtypeStruct((total, 4 * cells), BF16),
        ],
        scratch_shapes=scratch(lon, lon - 2),
        compiler_params=params(),
        name="first_half_inner",
    )(mix, east, north, field)
    whole1 = lambda *shape: pl.BlockSpec(shape, lambda: (0,) * len(shape))
    far = pl.BlockSpec(memory_space=pltpu.MemorySpace.HBM)
    forcing_scratch = [
        pltpu.VMEM((total, slots), BF16),
        pltpu.VMEM((8, slots), F32),
        pltpu.SMEM((2 * regions_of(capacity),), F32),
    ]
    own_w, own_e = pl.pallas_call(
        functools.partial(rim_kernel, lon=lon, levels=levels, tracers=tracers),
        in_specs=[
            whole1(rows, rows),
            whole1(levels * lon, lat),
            whole1(levels * lon, lat),
            whole1(fwd_rows, lat),
            whole1(bwd_rows, lat),
            whole1(total, 4 * cells),
            whole1(tiles, height, capacity),
        ],
        out_specs=[whole1(total, cells), whole1(total, cells)],
        out_shape=[jax.ShapeDtypeStruct((total, cells), BF16)] * 2,
        scratch_shapes=scratch(6 * HALO, 4 * HALO)
        + forcing_scratch
        + [pltpu.VMEM((total, 2 * cells), F32)],
        compiler_params=params(),
        name="rim",
    )(mix, east, north, fwd, bwd, near, got)
    far_w = lax.ppermute(own_e, "tile", ring)
    far_e = lax.ppermute(own_w, "tile", back)
    inner = pl.pallas_call(
        functools.partial(forcing_inner_kernel, lat=lat, levels=levels, tracers=tracers),
        in_specs=[whole1(tiles, height, capacity), far],
        out_specs=far,
        out_shape=jax.ShapeDtypeStruct((total, inner_width), BF16),
        scratch_shapes=forcing_scratch
        + [
            pltpu.VMEM((total, inner_width), F32),
            pltpu.VMEM((total, inner_width), BF16),
            pltpu.SemaphoreType.DMA((pairs - 2,)),
            pltpu.SemaphoreType.DMA((pairs - 2,)),
        ],
        compiler_params=params(),
        name="forcing_inner",
    )(got, middle)

    coefs, fields, mixed = scratch(lon + 2 * HALO, lon + 2 * HALO - 2)
    out = pl.pallas_call(
        functools.partial(second_half_kernel, lon=lon, levels=levels, total=total),
        in_specs=[whole1(rows, rows)] + [far] * 9,
        out_specs=far,
        out_shape=jax.ShapeDtypeStruct((total * lon, lat), F32),
        scratch_shapes=[
            pltpu.VMEM((levels * lon, lat), F32),
            pltpu.VMEM((levels * lon, lat), F32),
            pltpu.VMEM((fwd_rows, lat), BF16),
            pltpu.VMEM((bwd_rows, lat), BF16),
            coefs,
            pltpu.VMEM((total, (lon + 2 * HALO) * lat), BF16),
            mixed,
            pltpu.VMEM((total * lon, lat), F32),
            pltpu.SemaphoreType.DMA((4,)),
            pltpu.SemaphoreType.DMA((steps, 5)),
            pltpu.SemaphoreType.DMA((steps,)),
        ],
        compiler_params=params(),
        name="second_half",
    )(mix, east, north, fwd, bwd, far_w, own_w, inner, own_e, far_e)
    return out.reshape(tracers, levels, lon, lat)


def solution(mesh):
    in_specs = (
        P("ens", None, "tile", None),
        P("ens", "tile", None),
        P("ens", "tile", None),
        P(),
        P("ens", "tile"),
        P("ens", "tile"),
        P("tile", "ens"),
        P("ens", "tile"),
    )
    out_specs = P("ens", None, "tile", None)
    return jax.shard_map(
        per_device, mesh=mesh, in_specs=in_specs, out_specs=out_specs, check_vma=False
    )
```

```python
import functools

import jax
import jax.numpy as jnp
from jax import lax
from jax.experimental import pallas as pl
from jax.experimental.pallas import tpu as pltpu
from jax.sharding import PartitionSpec as P

F32 = jnp.float32
BF16 = jnp.bfloat16
GROUP = 2
HALO = 2
VMEM_BYTES = 20 * 1024 * 1024
VMEM = pltpu.MemorySpace.VMEM


def params(**more):
    return pltpu.CompilerParams(vmem_limit_bytes=VMEM_BYTES, **more)


def near_by(*arrays):
    return [pltpu.with_memory_space_constraint(array, VMEM) for array in arrays]


def away(array):
    return pltpu.with_memory_space_constraint(array, pltpu.MemorySpace.HBM)


def nt_dot(a, b):
    return lax.dot_general(a, b, (((1,), (1,)), ((), ())), preferred_element_type=F32)


def rows16(row):
    return jnp.broadcast_to(row, (16, row.shape[1])).astype(BF16)


def stacked(block, count):
    return jnp.concatenate([block] * count, axis=0)


def pack_kernel(
    kernel_ref, weight_ref, owner_ref, column_ref, out_ref, *, tiles, capacity, lat, pairs
):
    levels, pixels = kernel_ref.shape
    column = column_ref[...]
    longitude = column // lat
    line = lax.broadcasted_iota(jnp.int32, (8, pixels), 0)
    place = jnp.where(
        line == 0,
        (longitude + 1).astype(F32),
        jnp.where(line == 1, (column % lat).astype(F32), 0.0),
    )
    payload = jnp.concatenate(
        [kernel_ref[...].astype(F32), weight_ref[...].astype(F32), place], axis=0
    ).astype(BF16)
    classes = tiles * pairs
    named = owner_ref[...] * pairs + longitude // HALO
    block = min(256, pixels)

    def iota(shape, dim):
        return lax.broadcasted_iota(jnp.int32, shape, dim)

    def flags(mask):
        return mask.astype(F32).astype(BF16)

    upto = flags(iota((block, block), 0) <= iota((block, block), 1))
    carry = jnp.zeros((classes, 1), F32)
    members, counted = [], []
    for start in range(0, pixels, block):
        member = named[:, start : start + block] == iota((classes, block), 0)
        counts = jnp.dot(flags(member), upto, preferred_element_type=F32) + carry
        carry = counts[:, block - 1 : block]
        members.append(member)
        counted.append(counts)
    size = jnp.broadcast_to(carry, (classes, 128))
    row, other = iota((classes, classes), 0), iota((classes, classes), 1)
    same = row // pairs == other // pairs
    sizes = size.astype(BF16)
    before = jnp.dot(flags(same & (other < row)), sizes, preferred_element_type=F32)
    after = jnp.dot(flags(same & (other >= row)), sizes, preferred_element_type=F32)
    pair = iota((classes, 128), 0) % pairs
    slack = pair.astype(F32) * (capacity // pairs) - before
    shift = 1
    while shift < pairs:
        slack = jnp.where(pair >= shift, jnp.maximum(slack, pltpu.roll(slack, shift, 0)), slack)
        shift = 2 * shift
    begin = jnp.minimum(before + slack, capacity - after)[:, :1]
    gather = flags(iota((tiles, classes), 0) == iota((tiles, classes), 1) // pairs)
    ranks = [
        jnp.dot(
            gather,
            jnp.where(member, begin + counts, 0.0).astype(BF16),
            preferred_element_type=F32,
        )
        - 1.0
        for member, counts in zip(members, counted)
    ]
    ranks = jnp.concatenate(ranks, axis=1)
    slot = iota((capacity, pixels), 0).astype(F32).astype(BF16)
    for tile in range(tiles):
        rank = stacked(rows16(ranks[tile : tile + 1, :]), capacity // 16)
        chosen = jnp.where(slot == rank, jnp.ones_like(slot), jnp.zeros_like(slot))
        out_ref[tile] = nt_dot(payload, chosen).astype(BF16)


def both(ref, block, x, lon, levels):
    parts = [
        ref[pl.ds((t * levels + block * 8) * lon + x, 8, stride=lon), :] for t in range(GROUP)
    ]
    return jnp.concatenate(parts, axis=0).astype(BF16)


def edge_kernel(
    field_ref, east_ref, north_ref, level_mix_ref, fwd_ref, bwd_ref, mix_ref, *, lon, levels
):
    rows = GROUP * levels
    total = field_ref.shape[0] // lon
    for group in range(total // rows):
        view = field_ref.at[group * rows * lon : (group + 1) * rows * lon, :]
        for c in range(HALO):
            for block in range(levels // 8):
                spot = c * total + group * rows + block * 8 * GROUP
                at = slice(spot, spot + 8 * GROUP)
                fwd_ref[at, :] = both(view, block, lon - HALO + c, lon, levels)
                bwd_ref[at, :] = both(view, block, c, lon, levels)

    def put(out, place, ref, x):
        spot = HALO * total + place * (levels + 8)
        value = ref[pl.ds(x, levels, stride=lon), :]
        value = jnp.concatenate([value, jnp.zeros((8, value.shape[1]), F32)], axis=0)
        out[spot : spot + levels + 8, :] = value.astype(BF16)

    put(fwd_ref, 0, east_ref, lon - 2)
    put(fwd_ref, 1, east_ref, lon - 1)
    put(fwd_ref, 2, north_ref, lon - 1)
    put(bwd_ref, 0, east_ref, 0)
    put(bwd_ref, 1, north_ref, 0)
    row = lax.broadcasted_iota(jnp.int32, (rows, levels), 0)
    level = row // (8 * GROUP) * 8 + row % 8
    mine = level == lax.broadcasted_iota(jnp.int32, (rows, levels), 1)
    mix = jnp.zeros((rows, rows), F32)
    for t in range(GROUP):
        pick = (mine & (row // 8 % GROUP == t)).astype(F32).astype(BF16)
        mix = mix + nt_dot(nt_dot(pick, level_mix_ref[...]).astype(BF16), pick)
    mix_ref[...] = mix.astype(BF16)


def fill_coefs(east_ref, north_ref, edges, coef_ref, columns, lon, levels, total):
    lat = east_ref.shape[1]
    base = HALO * total

    def far(ref, place):
        spot = base + place * (levels + 8)
        return ref[spot : spot + levels + 8, :].astype(F32)[:levels]

    def own(ref, x):
        return ref[pl.ds(x, levels, stride=lon), :]

    def east(x):
        if x < 0:
            return far(edges[0], x + HALO)
        return own(east_ref, x) if x < lon else far(edges[1], 0)

    def north(x):
        if x < 0:
            return far(edges[0], 2)
        return own(north_ref, x) if x < lon else far(edges[1], 1)

    lane = lax.broadcasted_iota(jnp.int32, (levels, lat), 1)
    for i, x in enumerate(columns):
        at = slice(i * lat, (i + 1) * lat)
        face = jnp.where(lane < lat - 1, north(x), 0.0)
        to_east = jnp.maximum(east(x), 0.0)
        to_west = jnp.minimum(east(x - 1), 0.0)
        to_north = jnp.maximum(face, 0.0)
        to_south = pltpu.roll(jnp.minimum(face, 0.0), 1, 1)
        coef_ref[0, :, at] = (1.0 - to_east) + to_west + (to_south - to_north)
        coef_ref[1, :, at] = to_east
        coef_ref[2, :, at] = -to_west
        coef_ref[3, :, at] = to_north
        coef_ref[4, :, at] = -to_south


def stencil(mixed_ref, coef, start, count, lat, levels, emit):
    def column(e):
        return slice(e * lat, (e + 1) * lat)

    for block in range(levels // 8):
        lines = slice(block * 8, block * 8 + 8)
        tracer_rows = [
            slice(block * 8 * GROUP + 8 * t, block * 8 * GROUP + 8 * t + 8) for t in range(GROUP)
        ]
        left = [mixed_ref[r, column(start - 1)] for r in tracer_rows]
        centre = [mixed_ref[r, column(start)] for r in tracer_rows]
        for e in range(start, start + count):
            factor = [coef(j, lines, e) for j in range(5)]
            values = []
            for t, r in enumerate(tracer_rows):
                right = mixed_ref[r, column(e + 1)]
                value = (factor[0] * centre[t] + factor[1] * right) + (
                    factor[2] * left[t] + factor[3] * pltpu.roll(centre[t], lat - 1, 1)
                )
                values.append(value + factor[4] * pltpu.roll(centre[t], 1, 1))
                left[t], centre[t] = centre[t], right
            emit(block, e, values)


def two_steps(mix_ref, field_ref, mixed_ref, coef, start, count, lat, levels, put):
    def mix(lo, hi):
        for e in range(lo, hi, 2):
            at = slice(e * lat, (e + 2) * lat)
            mixed_ref[:, at] = jnp.dot(mix_ref[...], field_ref[:, at], preferred_element_type=F32)

    def keep(block, e, values):
        at = slice(block * 8 * GROUP, (block + 1) * 8 * GROUP)
        field_ref[at, e * lat : (e + 1) * lat] = jnp.concatenate(values, axis=0).astype(BF16)

    mix(start, start + count)
    stencil(mixed_ref, coef, start + 1, count - 2, lat, levels, keep)
    mix(start + 1, start + count - 1)
    stencil(mixed_ref, coef, start + 2, count - 4, lat, levels, put)


def factors(coef_ref, lat, place_of):
    def coef(j, lines, e):
        place = place_of(e)
        return coef_ref[j, lines, place * lat : (place + 1) * lat]

    return coef


def inner_kernel(
    mix_ref, east_ref, north_ref, in_ref, out_ref, near_ref, coef_hbm, coef_ref, field_ref,
    mixed_ref, coef_sem, *, lon, levels,
):
    lat = in_ref.shape[1]
    rows = GROUP * levels
    step = pl.program_id(0)
    base = pl.multiple_of(step * rows * lon, 16)
    source = in_ref.at[pl.ds(base, rows * lon), :]

    @pl.when(step == 0)
    def _():
        fill_coefs(east_ref, north_ref, None, coef_ref, range(1, lon - 1), lon, levels, 0)
        pltpu.make_async_copy(coef_ref, coef_hbm, coef_sem).start()

    for x in range(lon):
        for block in range(levels // 8):
            at = slice(block * 8 * GROUP, (block + 1) * 8 * GROUP)
            field_ref[at, x * lat : (x + 1) * lat] = both(source, block, x, lon, levels)
    side = 2 * HALO * lat
    mine = pl.ds(pl.multiple_of(step * rows, 16), rows)
    near_ref[mine, :side] = field_ref[:, :side]
    near_ref[mine, side:] = field_ref[:, lon * lat - side :]

    def put(block, e, values):
        for t, value in enumerate(values):
            row = block * 8 * GROUP + 8 * t
            out_ref[row : row + 8, (e - HALO) * lat : (e - HALO + 1) * lat] = value

    coef = factors(coef_ref, lat, lambda e: e - 1)
    two_steps(mix_ref, field_ref, mixed_ref, coef, 0, lon, lat, levels, put)

    @pl.when(step == pl.num_programs(0) - 1)
    def _():
        pltpu.make_async_copy(coef_ref, coef_hbm, coef_sem).wait()


def rim_kernel(
    mix_ref, east_ref, north_ref, fwd_ref, bwd_ref, near_ref, got_ref, west_out_ref, east_out_ref,
    coef_ref, weighted_ref, place_ref, field_ref, mixed_ref, range_ref, total_ref,
    *, lon, levels, tracers,
):
    total = near_ref.shape[0]
    lat = fwd_ref.shape[1]
    rows = GROUP * levels
    wide = 3 * HALO
    columns = list(range(1 - HALO, HALO + 1)) + list(range(lon - HALO - 1, lon + HALO - 1))
    fill_coefs(east_ref, north_ref, (fwd_ref, bwd_ref), coef_ref, columns, lon, levels, total)

    def group_of(group, carry):
        for c in range(HALO):
            at = pl.ds(pl.multiple_of(c * total + group * rows, 16), rows)
            field_ref[:, c * lat : (c + 1) * lat] = fwd_ref[at, :]
            e = wide + 2 * HALO + c
            field_ref[:, e * lat : (e + 1) * lat] = bwd_ref[at, :]
        side = 2 * HALO * lat
        mine = pl.ds(pl.multiple_of(group * rows, 16), rows)
        field_ref[:, HALO * lat : HALO * lat + side] = near_ref[mine, :side]
        field_ref[:, wide * lat : wide * lat + side] = near_ref[mine, side:]
        for half in range(2):
            start = half * wide

            def put(block, e, values):
                spot = (e - start - HALO + half * HALO) * lat
                for t, value in enumerate(values):
                    row = pl.multiple_of(group * rows + block * 8 * GROUP + 8 * t, 8)
                    total_ref[pl.ds(row, 8), spot : spot + lat] = value

            coef = factors(coef_ref, lat, lambda e: e - start - 1 + half * 2 * HALO)
            two_steps(mix_ref, field_ref, mixed_ref, coef, start, wide, lat, levels, put)
        return carry

    lax.fori_loop(0, total // rows, group_of, 0)
    weigh(got_ref, weighted_ref, place_ref, range_ref, lat, levels, tracers)
    cells = HALO * lat
    for side, out_ref in ((0, west_out_ref), (1, east_out_ref)):
        at = slice(side * cells, (side + 1) * cells)
        pair = side * (lon // HALO - 1)
        add_forcing(weighted_ref, place_ref, range_ref, total_ref, at, float(pair * cells))
        out_ref[...] = total_ref[:, at].astype(BF16)


def second_half_kernel(
    mix_ref, inner_coef_ref, rim_coef_ref, far_w_ref, own_w_ref, inner_ref, own_e_ref, far_e_ref,
    out_hbm, field_ref, mixed_ref, result_ref, out_sems, *, lon, levels,
):
    lat = out_hbm.shape[1]
    rows = GROUP * levels
    groups = far_w_ref.shape[0] // rows

    def coef(j, lines, e):
        x = e - HALO
        if x < 1:
            ref, place = rim_coef_ref, x + HALO - 1
        elif x < lon - 1:
            ref, place = inner_coef_ref, x - 1
        else:
            ref, place = rim_coef_ref, x - (lon - HALO - 1) + 2 * HALO
        return ref[j, lines, place * lat : (place + 1) * lat]

    def leave(group):
        at = pl.ds(pl.multiple_of(group * rows * lon, 16), rows * lon)
        return pltpu.make_async_copy(result_ref.at[at, :], out_hbm.at[at, :], out_sems.at[group])

    def group_of(group, carry):
        mine = pl.ds(pl.multiple_of(group * rows, 16), rows)
        spot = 0
        for ref in (far_w_ref, own_w_ref, inner_ref, own_e_ref, far_e_ref):
            width = ref.shape[1]
            field_ref[:, spot : spot + width] = ref[mine, :]
            spot = spot + width
        base = pl.multiple_of(group * rows * lon, 16)
        result = result_ref.at[pl.ds(base, rows * lon), :]

        def put(block, e, values):
            for t, value in enumerate(values):
                first = (t * levels + block * 8) * lon + e - HALO
                result[pl.ds(first, 8, stride=lon), :] = value

        two_steps(mix_ref, field_ref, mixed_ref, coef, 0, lon + 2 * HALO, lat, levels, put)
        leave(group).start()
        return carry

    lax.fori_loop(0, groups, group_of, 0)
    for group in range(groups):
        leave(group).wait()


def regions_of(capacity):
    return capacity // 64 if capacity % 128 == 0 else 1


def regroup(got_ref, store):
    tiles, height, capacity = got_ref.shape
    if regions_of(capacity) == 1:
        for tile in range(tiles):
            store(tile * capacity, got_ref[tile].astype(F32))
        return
    low = lax.broadcasted_iota(jnp.int32, (height, 128), 1) < 64
    for tile in range(0, tiles, 2):
        for half in range(capacity // 128):
            at = slice(half * 128, half * 128 + 128)
            one, two = got_ref[tile, :, at].astype(F32), got_ref[tile + 1, :, at].astype(F32)
            spot = 2 * half * tiles * 64 + tile * 64
            store(spot, jnp.where(low, one, pltpu.roll(two, 64, 1)))
            store(spot + tiles * 64, jnp.where(low, pltpu.roll(one, 64, 1), two))


def weigh(got_ref, weighted_ref, place_ref, range_ref, lat, levels, tracers):
    def store(spot, got):
        at = slice(spot, spot + got.shape[1])
        row = 0
        for t in range(0, tracers, GROUP):
            for block in range(0, levels, 8):
                kernel = got[block : block + 8]
                pieces = [
                    kernel * got[levels + j : levels + j + 1, :] for j in range(t, t + GROUP)
                ]
                value = jnp.concatenate(pieces, axis=0).astype(BF16)
                weighted_ref[row : row + 8 * GROUP, at] = value
                row = row + 8 * GROUP
        first = levels + tracers
        column = (got[first : first + 1, :] - 1.0) * lat + got[first + 1 : first + 2, :]
        place_ref[:, at] = jnp.broadcast_to(column, (8, got.shape[1]))

    regroup(got_ref, store)
    span(place_ref, range_ref)


def span(place_ref, range_ref):
    parts = range_ref.shape[0] // 2
    wide = place_ref.shape[1] // parts
    for part in range(parts):
        place = place_ref[:, part * wide : (part + 1) * wide]
        range_ref[2 * part] = jnp.min(jnp.where(place < 0.0, 1e6, place))
        range_ref[2 * part + 1] = jnp.max(place)


def add_forcing(weighted_ref, place_ref, range_ref, total_ref, columns, offset):
    cells = total_ref[:, columns].shape[1]
    parts = range_ref.shape[0] // 2
    wide = weighted_ref.shape[1] // parts
    for part in range(parts):
        held = (range_ref[2 * part] < offset + cells) & (range_ref[2 * part + 1] >= offset)

        @pl.when(held)
        def _():
            at = slice(part * wide, (part + 1) * wide)
            key = rows16(place_ref[0:1, at] - offset)
            cell = lax.broadcasted_iota(jnp.int32, (cells, wide), 0).astype(F32).astype(BF16)
            hit = cell == stacked(key, cells // 16)
            one_hot = jnp.where(hit, jnp.ones_like(cell), jnp.zeros_like(cell))
            total_ref[:, columns] += nt_dot(weighted_ref[:, at], one_hot)


def forcing_inner_kernel(
    weighted_ref, place_ref, field_ref, out_ref, range_ref, total_ref, *, lat
):
    cells = HALO * lat
    span(place_ref, range_ref)

    def pair_of(i, carry):
        at = pl.ds(pl.multiple_of(i * cells, cells), cells)
        total_ref[...] = field_ref[:, at]
        offset = ((i + 1) * cells).astype(F32)
        add_forcing(weighted_ref, place_ref, range_ref, total_ref, slice(0, cells), offset)
        out_ref[:, at] = total_ref[...].astype(BF16)
        return carry

    lax.fori_loop(0, field_ref.shape[1] // cells, pair_of, 0)


def per_device(
    adjoint_in,
    east_courant,
    north_courant,
    level_mix,
    avg_kernel,
    pixel_weight,
    pixel_owner,
    pixel_column,
):
    tracers, levels, lon, lat = adjoint_in.shape
    pixels = avg_kernel.shape[1]
    tiles = lax.axis_size("tile")
    capacity = 4 * pixels // tiles
    slots = tiles * capacity
    total = tracers * levels
    steps = tracers // GROUP
    rows = GROUP * levels
    ring = [(i, (i + 1) % tiles) for i in range(tiles)]
    back = [((i + 1) % tiles, i) for i in range(tiles)]

    field = adjoint_in.reshape(total * lon, lat)
    east = east_courant.reshape(levels * lon, lat)
    north = north_courant.reshape(levels * lon, lat)
    here = pl.BlockSpec(memory_space=VMEM)
    far = pl.BlockSpec(memory_space=pltpu.MemorySpace.HBM)
    pairs = lon // HALO
    height = levels + tracers + 8
    payload = pl.pallas_call(
        functools.partial(pack_kernel, tiles=tiles, capacity=capacity, lat=lat, pairs=pairs),
        out_specs=here,
        out_shape=pltpu.VMEM((tiles, height, capacity), BF16),
        compiler_params=params(),
        name="pack",
    )(
        away(avg_kernel),
        away(pixel_weight),
        away(pixel_owner.reshape(1, pixels)),
        away(pixel_column),
    )
    got = lax.all_to_all(payload, "tile", split_axis=0, concat_axis=0, tiled=True)

    fwd_rows = HALO * total + 3 * (levels + 8)
    bwd_rows = HALO * total + 2 * (levels + 8)
    fwd, bwd, mix = pl.pallas_call(
        functools.partial(edge_kernel, lon=lon, levels=levels),
        in_specs=[here, here, here, pl.BlockSpec((levels, levels), lambda: (0, 0))],
        out_specs=[here] * 3,
        out_shape=[
            pltpu.VMEM((fwd_rows, lat), BF16),
            pltpu.VMEM((bwd_rows, lat), BF16),
            pltpu.VMEM((rows, rows), BF16),
        ],
        compiler_params=params(),
        name="edges",
    )(*near_by(field, east, north), away(level_mix))
    fwd = lax.ppermute(fwd, "tile", ring)
    bwd = lax.ppermute(bwd, "tile", back)

    def scratch(columns):
        return [
            pltpu.VMEM((rows, columns * lat), BF16),
            pltpu.VMEM((rows, columns * lat), F32),
        ]

    cells = HALO * lat
    inner_width = (lon - 2 * HALO) * lat
    middle, near, inner_coef = pl.pallas_call(
        functools.partial(inner_kernel, lon=lon, levels=levels),
        grid=(steps,),
        in_specs=[here] * 4,
        out_specs=[pl.BlockSpec((rows, inner_width), lambda i: (i, 0)), here, far],
        out_shape=[
            pltpu.HBM((total, inner_width), F32),
            pltpu.VMEM((total, 4 * cells), BF16),
            pltpu.HBM((5, levels, (lon - 2) * lat), F32),
        ],
        scratch_shapes=[pltpu.VMEM((5, levels, (lon - 2) * lat), F32)]
        + scratch(lon)
        + [pltpu.SemaphoreType.DMA],
        compiler_params=params(),
        name="first_half_inner",
    )(*near_by(mix, east, north, field))

    ranges = pltpu.SMEM((2 * regions_of(capacity),), F32)
    own_w, own_e, rim_coef, weighted, place = pl.pallas_call(
        functools.partial(rim_kernel, lon=lon, levels=levels, tracers=tracers),
        in_specs=[here] * 7,
        out_specs=[here] * 5,
        out_shape=[
            pltpu.VMEM((total, cells), BF16),
            pltpu.VMEM((total, cells), BF16),
            pltpu.VMEM((5, levels, 4 * HALO * lat), F32),
            pltpu.VMEM((total, slots), BF16),
            pltpu.VMEM((8, slots), F32),
        ],
        scratch_shapes=scratch(6 * HALO) + [ranges, pltpu.VMEM((total, 2 * cells), F32)],
        compiler_params=params(),
        name="rim",
    )(*near_by(mix, east, north, fwd, bwd, near, got))
    far_w = lax.ppermute(own_e, "tile", ring)
    far_e = lax.ppermute(own_w, "tile", back)
    inner = pl.pallas_call(
        functools.partial(forcing_inner_kernel, lat=lat),
        in_specs=[here] * 3,
        out_specs=here,
        out_shape=pltpu.VMEM((total, inner_width), BF16),
        scratch_shapes=[ranges, pltpu.VMEM((total, cells), F32)],
        compiler_params=params(),
        name="forcing_inner",
    )(*near_by(weighted, place, middle))

    out = pl.pallas_call(
        functools.partial(second_half_kernel, lon=lon, levels=levels),
        in_specs=[here] * 8,
        out_specs=far,
        out_shape=jax.ShapeDtypeStruct((total * lon, lat), F32),
        scratch_shapes=scratch(lon + 2 * HALO)
        + [pltpu.VMEM((total * lon, lat), F32), pltpu.SemaphoreType.DMA((steps,))],
        compiler_params=params(),
        name="second_half",
    )(*near_by(mix, inner_coef, rim_coef, far_w, own_w, inner, own_e, far_e))
    return out.reshape(tracers, levels, lon, lat)


def solution(mesh):
    in_specs = (
        P("ens", None, "tile", None),
        P("ens", "tile", None),
        P("ens", "tile", None),
        P(),
        P("ens", "tile"),
        P("ens", "tile"),
        P("tile", "ens"),
        P("ens", "tile"),
    )
    out_specs = P("ens", None, "tile", None)
    return jax.shard_map(
        per_device, mesh=mesh, in_specs=in_specs, out_specs=out_specs, check_vma=False
    )
```

```python
import functools

import jax
import jax.numpy as jnp
from jax import lax
from jax.experimental import pallas as pl
from jax.experimental.pallas import tpu as pltpu
from jax.sharding import PartitionSpec as P

F32 = jnp.float32
BF16 = jnp.bfloat16
GROUP = 2
RIM_TOGETHER = 2
TOGETHER = 2
HALO = 2
VMEM_BYTES = 20 * 1024 * 1024
VMEM = pltpu.MemorySpace.VMEM


def params(**more):
    return pltpu.CompilerParams(vmem_limit_bytes=VMEM_BYTES, **more)


def near_by(*arrays):
    return [pltpu.with_memory_space_constraint(array, VMEM) for array in arrays]


def away(array):
    return pltpu.with_memory_space_constraint(array, pltpu.MemorySpace.HBM)


def nt_dot(a, b):
    return lax.dot_general(a, b, (((1,), (1,)), ((), ())), preferred_element_type=F32)


def rows16(row):
    return jnp.broadcast_to(row, (16, row.shape[1])).astype(BF16)


def stacked(block, count):
    return jnp.concatenate([block] * count, axis=0)


def pack_kernel(
    kernel_ref, weight_ref, owner_ref, column_ref, out_ref, *, tiles, capacity, lat, pairs
):
    levels, pixels = kernel_ref.shape
    column = column_ref[...]
    longitude = column // lat
    line = lax.broadcasted_iota(jnp.int32, (8, pixels), 0)
    place = jnp.where(
        line == 0,
        (longitude + 1).astype(F32),
        jnp.where(line == 1, (column % lat).astype(F32), 0.0),
    )
    payload = jnp.concatenate(
        [kernel_ref[...].astype(F32), weight_ref[...].astype(F32), place], axis=0
    ).astype(BF16)
    classes = tiles * pairs
    named = owner_ref[...] * pairs + longitude // HALO
    block = min(256, pixels)

    def iota(shape, dim):
        return lax.broadcasted_iota(jnp.int32, shape, dim)

    def flags(mask):
        return mask.astype(F32).astype(BF16)

    upto = flags(iota((block, block), 0) <= iota((block, block), 1))
    carry = jnp.zeros((classes, 1), F32)
    members, counted = [], []
    for start in range(0, pixels, block):
        member = named[:, start : start + block] == iota((classes, block), 0)
        counts = jnp.dot(flags(member), upto, preferred_element_type=F32) + carry
        carry = counts[:, block - 1 : block]
        members.append(member)
        counted.append(counts)
    size = jnp.broadcast_to(carry, (classes, 128))
    row, other = iota((classes, classes), 0), iota((classes, classes), 1)
    same = row // pairs == other // pairs
    sizes = size.astype(BF16)
    before = jnp.dot(flags(same & (other < row)), sizes, preferred_element_type=F32)
    after = jnp.dot(flags(same & (other >= row)), sizes, preferred_element_type=F32)
    pair = iota((classes, 128), 0) % pairs
    slack = pair.astype(F32) * (capacity // pairs) - before
    shift = 1
    while shift < pairs:
        slack = jnp.where(pair >= shift, jnp.maximum(slack, pltpu.roll(slack, shift, 0)), slack)
        shift = 2 * shift
    begin = jnp.minimum(before + slack, capacity - after)[:, :1]
    gather = flags(iota((tiles, classes), 0) == iota((tiles, classes), 1) // pairs)
    ranks = [
        jnp.dot(
            gather,
            jnp.where(member, begin + counts, 0.0).astype(BF16),
            preferred_element_type=F32,
        )
        - 1.0
        for member, counts in zip(members, counted)
    ]
    ranks = jnp.concatenate(ranks, axis=1)
    slot = iota((capacity, pixels), 0).astype(F32).astype(BF16)
    for tile in range(tiles):
        rank = stacked(rows16(ranks[tile : tile + 1, :]), capacity // 16)
        chosen = jnp.where(slot == rank, jnp.ones_like(slot), jnp.zeros_like(slot))
        out_ref[tile] = nt_dot(payload, chosen).astype(BF16)


def both(ref, block, x, lon, levels):
    parts = [
        ref[pl.ds((t * levels + block * 8) * lon + x, 8, stride=lon), :] for t in range(GROUP)
    ]
    return jnp.concatenate(parts, axis=0).astype(BF16)


def edge_kernel(
    field_ref, east_ref, north_ref, level_mix_ref, fwd_ref, bwd_ref, mix_ref, *, lon, levels
):
    rows = GROUP * levels
    total = field_ref.shape[0] // lon
    for group in range(total // rows):
        view = field_ref.at[group * rows * lon : (group + 1) * rows * lon, :]
        for c in range(HALO):
            for block in range(levels // 8):
                spot = c * total + group * rows + block * 8 * GROUP
                at = slice(spot, spot + 8 * GROUP)
                fwd_ref[at, :] = both(view, block, lon - HALO + c, lon, levels)
                bwd_ref[at, :] = both(view, block, c, lon, levels)

    def put(out, place, ref, x):
        spot = HALO * total + place * (levels + 8)
        value = ref[pl.ds(x, levels, stride=lon), :]
        value = jnp.concatenate([value, jnp.zeros((8, value.shape[1]), F32)], axis=0)
        out[spot : spot + levels + 8, :] = value.astype(BF16)

    put(fwd_ref, 0, east_ref, lon - 2)
    put(fwd_ref, 1, east_ref, lon - 1)
    put(fwd_ref, 2, north_ref, lon - 1)
    put(bwd_ref, 0, east_ref, 0)
    put(bwd_ref, 1, north_ref, 0)
    row = lax.broadcasted_iota(jnp.int32, (rows, levels), 0)
    level = row // (8 * GROUP) * 8 + row % 8
    mine = level == lax.broadcasted_iota(jnp.int32, (rows, levels), 1)
    mix = jnp.zeros((rows, rows), F32)
    for t in range(GROUP):
        pick = (mine & (row // 8 % GROUP == t)).astype(F32).astype(BF16)
        mix = mix + nt_dot(nt_dot(pick, level_mix_ref[...]).astype(BF16), pick)
    mix_ref[...] = mix.astype(BF16)


def fill_coefs(east_ref, north_ref, edges, coef_ref, columns, lon, levels, total):
    lat = east_ref.shape[1]
    base = HALO * total

    def far(ref, place):
        spot = base + place * (levels + 8)
        return ref[spot : spot + levels + 8, :].astype(F32)[:levels]

    def own(ref, x):
        return ref[pl.ds(x, levels, stride=lon), :]

    def east(x):
        if x < 0:
            return far(edges[0], x + HALO)
        return own(east_ref, x) if x < lon else far(edges[1], 0)

    def north(x):
        if x < 0:
            return far(edges[0], 2)
        return own(north_ref, x) if x < lon else far(edges[1], 1)

    lane = lax.broadcasted_iota(jnp.int32, (levels, lat), 1)
    for i, x in enumerate(columns):
        at = slice(i * lat, (i + 1) * lat)
        face = jnp.where(lane < lat - 1, north(x), 0.0)
        to_east = jnp.maximum(east(x), 0.0)
        to_west = jnp.minimum(east(x - 1), 0.0)
        to_north = jnp.maximum(face, 0.0)
        to_south = pltpu.roll(jnp.minimum(face, 0.0), 1, 1)
        coef_ref[0, :, at] = (1.0 - to_east) + to_west + (to_south - to_north)
        coef_ref[1, :, at] = to_east
        coef_ref[2, :, at] = -to_west
        coef_ref[3, :, at] = to_north
        coef_ref[4, :, at] = -to_south


def stencil(mixed_ref, coef, start, count, lat, levels, emit):
    def column(e):
        return slice(e * lat, (e + 1) * lat)

    for block in range(levels // 8):
        lines = slice(block * 8, block * 8 + 8)
        tracer_rows = [
            slice(block * 8 * GROUP + 8 * t, block * 8 * GROUP + 8 * t + 8) for t in range(GROUP)
        ]
        left = [mixed_ref[r, column(start - 1)] for r in tracer_rows]
        centre = [mixed_ref[r, column(start)] for r in tracer_rows]
        for e in range(start, start + count):
            factor = [coef(j, lines, e) for j in range(5)]
            values = []
            for t, r in enumerate(tracer_rows):
                right = mixed_ref[r, column(e + 1)]
                value = (factor[0] * centre[t] + factor[1] * right) + (
                    factor[2] * left[t] + factor[3] * pltpu.roll(centre[t], lat - 1, 1)
                )
                values.append(value + factor[4] * pltpu.roll(centre[t], 1, 1))
                left[t], centre[t] = centre[t], right
            emit(block, e, values)


def two_steps(mix_ref, levels, lat, segments):
    def mix(field_ref, mixed_ref, lo, hi):
        for e in range(lo, hi, 2):
            at = slice(e * lat, (e + 2) * lat)
            mixed_ref[:, at] = jnp.dot(mix_ref[...], field_ref[:, at], preferred_element_type=F32)

    for field_ref, mixed_ref, _, start, count, _ in segments:
        mix(field_ref, mixed_ref, start, start + count)
    for field_ref, mixed_ref, coef, start, count, _ in segments:

        def keep(block, e, values):
            at = slice(block * 8 * GROUP, (block + 1) * 8 * GROUP)
            field_ref[at, e * lat : (e + 1) * lat] = jnp.concatenate(values, axis=0).astype(BF16)

        stencil(mixed_ref, coef, start + 1, count - 2, lat, levels, keep)
    for field_ref, mixed_ref, _, start, count, _ in segments:
        mix(field_ref, mixed_ref, start + 1, start + count - 1)
    for field_ref, mixed_ref, coef, start, count, put in segments:
        stencil(mixed_ref, coef, start + 2, count - 4, lat, levels, put)


def factors(coef_ref, lat, place_of):
    def coef(j, lines, e):
        place = place_of(e)
        return coef_ref[j, lines, place * lat : (place + 1) * lat]

    return coef


def inner_kernel(
    mix_ref, east_ref, north_ref, in_ref, out_ref, near_ref, coef_hbm, coef_ref, field_ref,
    mixed_ref, coef_sem, *, lon, levels,
):
    lat = in_ref.shape[1]
    rows = GROUP * levels
    step = pl.program_id(0)
    base = pl.multiple_of(step * rows * lon, 16)
    source = in_ref.at[pl.ds(base, rows * lon), :]

    @pl.when(step == 0)
    def _():
        fill_coefs(east_ref, north_ref, None, coef_ref, range(1, lon - 1), lon, levels, 0)
        pltpu.make_async_copy(coef_ref, coef_hbm, coef_sem).start()

    for x in range(lon):
        for block in range(levels // 8):
            at = slice(block * 8 * GROUP, (block + 1) * 8 * GROUP)
            field_ref[at, x * lat : (x + 1) * lat] = both(source, block, x, lon, levels)
    side = 2 * HALO * lat
    mine = pl.ds(pl.multiple_of(step * rows, 16), rows)
    near_ref[mine, :side] = field_ref[:, :side]
    near_ref[mine, side:] = field_ref[:, lon * lat - side :]

    def put(block, e, values):
        for t, value in enumerate(values):
            row = block * 8 * GROUP + 8 * t
            out_ref[row : row + 8, (e - HALO) * lat : (e - HALO + 1) * lat] = value

    coef = factors(coef_ref, lat, lambda e: e - 1)
    two_steps(mix_ref, levels, lat, [(field_ref, mixed_ref, coef, 0, lon, put)])

    @pl.when(step == pl.num_programs(0) - 1)
    def _():
        pltpu.make_async_copy(coef_ref, coef_hbm, coef_sem).wait()


def rim_kernel(
    mix_ref, east_ref, north_ref, fwd_ref, near_ref, got_ref, bwd_hbm, west_out_ref, east_out_ref,
    coef_ref, weighted_ref, place_ref, field_ref, mixed_ref, range_ref, total_ref, bwd_ref, bwd_sem,
    *, lon, levels, tracers,
):
    copy = pltpu.make_async_copy(bwd_hbm, bwd_ref, bwd_sem)
    copy.start()
    total = near_ref.shape[0]
    lat = fwd_ref.shape[1]
    rows = GROUP * levels
    wide = 3 * HALO
    weigh(got_ref, weighted_ref, place_ref, range_ref, lat, levels, tracers)
    copy.wait()
    columns = list(range(1 - HALO, HALO + 1)) + list(range(lon - HALO - 1, lon + HALO - 1))
    fill_coefs(east_ref, north_ref, (fwd_ref, bwd_ref), coef_ref, columns, lon, levels, total)
    together = field_ref.shape[0]

    def segment(group, slot, half):
        field, mixed = field_ref.at[slot], mixed_ref.at[slot]
        start = half * wide

        def put(block, e, values):
            spot = (e - start - HALO + half * HALO) * lat
            for t, value in enumerate(values):
                row = pl.multiple_of(group * rows + block * 8 * GROUP + 8 * t, 8)
                total_ref[pl.ds(row, 8), spot : spot + lat] = value

        coef = factors(coef_ref, lat, lambda e: e - start - 1 + half * 2 * HALO)
        return field, mixed, coef, start, wide, put

    def groups_of(i, carry):
        segments = []
        for slot in range(together):
            group = i * together + slot
            for c in range(HALO):
                at = pl.ds(pl.multiple_of(c * total + group * rows, 16), rows)
                field_ref[slot, :, c * lat : (c + 1) * lat] = fwd_ref[at, :]
                e = wide + 2 * HALO + c
                field_ref[slot, :, e * lat : (e + 1) * lat] = bwd_ref[at, :]
            side = 2 * HALO * lat
            mine = pl.ds(pl.multiple_of(group * rows, 16), rows)
            field_ref[slot, :, HALO * lat : HALO * lat + side] = near_ref[mine, :side]
            field_ref[slot, :, wide * lat : wide * lat + side] = near_ref[mine, side:]
            segments = segments + [segment(group, slot, half) for half in range(2)]
        two_steps(mix_ref, levels, lat, segments)
        return carry

    lax.fori_loop(0, total // rows // together, groups_of, 0)
    cells = HALO * lat
    for side, out_ref in ((0, west_out_ref), (1, east_out_ref)):
        at = slice(side * cells, (side + 1) * cells)
        pair = side * (lon // HALO - 1)
        add_forcing(weighted_ref, place_ref, range_ref, total_ref, at, float(pair * cells))
        out_ref[...] = total_ref[:, at].astype(BF16)


def second_half_kernel(
    mix_ref, inner_coef_ref, rim_coef_ref, far_w_ref, own_w_ref, inner_ref, own_e_ref, far_e_ref,
    out_hbm, field_ref, mixed_ref, result_ref, out_sems, *, lon, levels,
):
    lat = out_hbm.shape[1]
    rows = GROUP * levels
    groups = far_w_ref.shape[0] // rows

    def coef(j, lines, e):
        x = e - HALO
        if x < 1:
            ref, place = rim_coef_ref, x + HALO - 1
        elif x < lon - 1:
            ref, place = inner_coef_ref, x - 1
        else:
            ref, place = rim_coef_ref, x - (lon - HALO - 1) + 2 * HALO
        return ref[j, lines, place * lat : (place + 1) * lat]

    def leave(group):
        at = pl.ds(pl.multiple_of(group * rows * lon, 16), rows * lon)
        return pltpu.make_async_copy(result_ref.at[at, :], out_hbm.at[at, :], out_sems.at[group])

    together = field_ref.shape[0]

    def segment(group, slot):
        field = field_ref.at[slot]
        mine = pl.ds(pl.multiple_of(group * rows, 16), rows)
        spot = 0
        for ref in (far_w_ref, own_w_ref, inner_ref, own_e_ref, far_e_ref):
            width = ref.shape[1]
            field[:, spot : spot + width] = ref[mine, :]
            spot = spot + width
        base = pl.multiple_of(group * rows * lon, 16)
        result = result_ref.at[pl.ds(base, rows * lon), :]

        def put(block, e, values):
            for t, value in enumerate(values):
                first = (t * levels + block * 8) * lon + e - HALO
                result[pl.ds(first, 8, stride=lon), :] = value

        return field, mixed_ref.at[slot], coef, 0, lon + 2 * HALO, put

    def groups_of(i, carry):
        mine = [i * together + slot for slot in range(together)]
        two_steps(mix_ref, levels, lat, [segment(group, slot) for slot, group in enumerate(mine)])
        for group in mine:
            leave(group).start()
        return carry

    lax.fori_loop(0, groups // together, groups_of, 0)
    for group in range(groups):
        leave(group).wait()


def regions_of(capacity):
    return capacity // 64 if capacity % 128 == 0 else 1


def regroup(got_ref, store):
    tiles, height, capacity = got_ref.shape
    if regions_of(capacity) == 1:
        for tile in range(tiles):
            store(tile * capacity, got_ref[tile].astype(F32))
        return
    low = lax.broadcasted_iota(jnp.int32, (height, 128), 1) < 64
    for tile in range(0, tiles, 2):
        for half in range(capacity // 128):
            at = slice(half * 128, half * 128 + 128)
            one, two = got_ref[tile, :, at].astype(F32), got_ref[tile + 1, :, at].astype(F32)
            spot = 2 * half * tiles * 64 + tile * 64
            store(spot, jnp.where(low, one, pltpu.roll(two, 64, 1)))
            store(spot + tiles * 64, jnp.where(low, pltpu.roll(one, 64, 1), two))


def weigh(got_ref, weighted_ref, place_ref, range_ref, lat, levels, tracers):
    def store(spot, got):
        at = slice(spot, spot + got.shape[1])
        row = 0
        for t in range(0, tracers, GROUP):
            for block in range(0, levels, 8):
                kernel = got[block : block + 8]
                pieces = [
                    kernel * got[levels + j : levels + j + 1, :] for j in range(t, t + GROUP)
                ]
                value = jnp.concatenate(pieces, axis=0).astype(BF16)
                weighted_ref[row : row + 8 * GROUP, at] = value
                row = row + 8 * GROUP
        first = levels + tracers
        column = (got[first : first + 1, :] - 1.0) * lat + got[first + 1 : first + 2, :]
        place_ref[:, at] = jnp.broadcast_to(column, (8, got.shape[1]))

    regroup(got_ref, store)
    span(place_ref, range_ref)


def span(place_ref, range_ref):
    parts = range_ref.shape[0] // 2
    wide = place_ref.shape[1] // parts
    for part in range(parts):
        place = place_ref[:, part * wide : (part + 1) * wide]
        range_ref[2 * part] = jnp.min(jnp.where(place < 0.0, 1e6, place))
        range_ref[2 * part + 1] = jnp.max(place)


def add_forcing(weighted_ref, place_ref, range_ref, total_ref, columns, offset):
    cells = total_ref[:, columns].shape[1]
    parts = range_ref.shape[0] // 2
    wide = weighted_ref.shape[1] // parts
    for part in range(parts):
        held = (range_ref[2 * part] < offset + cells) & (range_ref[2 * part + 1] >= offset)

        @pl.when(held)
        def _():
            at = slice(part * wide, (part + 1) * wide)
            key = rows16(place_ref[0:1, at] - offset)
            cell = lax.broadcasted_iota(jnp.int32, (cells, wide), 0).astype(F32).astype(BF16)
            hit = cell == stacked(key, cells // 16)
            one_hot = jnp.where(hit, jnp.ones_like(cell), jnp.zeros_like(cell))
            total_ref[:, columns] += nt_dot(weighted_ref[:, at], one_hot)


def forcing_inner_kernel(
    weighted_ref, place_ref, field_ref, out_ref, range_ref, total_ref, *, lat
):
    cells = HALO * lat
    span(place_ref, range_ref)

    def pair_of(i, carry):
        at = pl.ds(pl.multiple_of(i * cells, cells), cells)
        total_ref[...] = field_ref[:, at]
        offset = ((i + 1) * cells).astype(F32)
        add_forcing(weighted_ref, place_ref, range_ref, total_ref, slice(0, cells), offset)
        out_ref[:, at] = total_ref[...].astype(BF16)
        return carry

    lax.fori_loop(0, field_ref.shape[1] // cells, pair_of, 0)


def per_device(
    adjoint_in,
    east_courant,
    north_courant,
    level_mix,
    avg_kernel,
    pixel_weight,
    pixel_owner,
    pixel_column,
):
    tracers, levels, lon, lat = adjoint_in.shape
    pixels = avg_kernel.shape[1]
    tiles = lax.axis_size("tile")
    capacity = 4 * pixels // tiles
    slots = tiles * capacity
    total = tracers * levels
    steps = tracers // GROUP
    rows = GROUP * levels
    ring = [(i, (i + 1) % tiles) for i in range(tiles)]
    back = [((i + 1) % tiles, i) for i in range(tiles)]

    field = adjoint_in.reshape(total * lon, lat)
    east = east_courant.reshape(levels * lon, lat)
    north = north_courant.reshape(levels * lon, lat)
    here = pl.BlockSpec(memory_space=VMEM)
    far = pl.BlockSpec(memory_space=pltpu.MemorySpace.HBM)
    pairs = lon // HALO
    height = levels + tracers + 8
    payload = pl.pallas_call(
        functools.partial(pack_kernel, tiles=tiles, capacity=capacity, lat=lat, pairs=pairs),
        out_specs=here,
        out_shape=pltpu.VMEM((tiles, height, capacity), BF16),
        compiler_params=params(),
        name="pack",
    )(
        away(avg_kernel),
        away(pixel_weight),
        away(pixel_owner.reshape(1, pixels)),
        away(pixel_column),
    )
    got = lax.all_to_all(payload, "tile", split_axis=0, concat_axis=0, tiled=True)

    fwd_rows = HALO * total + 3 * (levels + 8)
    bwd_rows = HALO * total + 2 * (levels + 8)
    fwd, bwd, mix = pl.pallas_call(
        functools.partial(edge_kernel, lon=lon, levels=levels),
        in_specs=[here, here, here, pl.BlockSpec((levels, levels), lambda: (0, 0))],
        out_specs=[here] * 3,
        out_shape=[
            pltpu.VMEM((fwd_rows, lat), BF16),
            pltpu.VMEM((bwd_rows, lat), BF16),
            pltpu.VMEM((rows, rows), BF16),
        ],
        compiler_params=params(),
        name="edges",
    )(*near_by(field, east, north), away(level_mix))
    fwd = lax.ppermute(fwd, "tile", ring)
    bwd = lax.ppermute(bwd, "tile", back)

    def scratch(columns, *together):
        return [
            pltpu.VMEM((*together, rows, columns * lat), BF16),
            pltpu.VMEM((*together, rows, columns * lat), F32),
        ]

    cells = HALO * lat
    inner_width = (lon - 2 * HALO) * lat
    middle, near, inner_coef = pl.pallas_call(
        functools.partial(inner_kernel, lon=lon, levels=levels),
        grid=(steps,),
        in_specs=[here] * 4,
        out_specs=[pl.BlockSpec((rows, inner_width), lambda i: (i, 0)), here, far],
        out_shape=[
            pltpu.HBM((total, inner_width), F32),
            pltpu.VMEM((total, 4 * cells), BF16),
            pltpu.HBM((5, levels, (lon - 2) * lat), F32),
        ],
        scratch_shapes=[pltpu.VMEM((5, levels, (lon - 2) * lat), F32)]
        + scratch(lon)
        + [pltpu.SemaphoreType.DMA],
        compiler_params=params(),
        name="first_half_inner",
    )(*near_by(mix, east, north, field))

    ranges = pltpu.SMEM((2 * regions_of(capacity),), F32)
    own_w, own_e, rim_coef, weighted, place = pl.pallas_call(
        functools.partial(rim_kernel, lon=lon, levels=levels, tracers=tracers),
        in_specs=[here] * 6 + [far],
        out_specs=[here] * 5,
        out_shape=[
            pltpu.VMEM((total, cells), BF16),
            pltpu.VMEM((total, cells), BF16),
            pltpu.VMEM((5, levels, 4 * HALO * lat), F32),
            pltpu.VMEM((total, slots), BF16),
            pltpu.VMEM((8, slots), F32),
        ],
        scratch_shapes=scratch(6 * HALO, RIM_TOGETHER)
        + [
            ranges,
            pltpu.VMEM((total, 2 * cells), F32),
            pltpu.VMEM((bwd_rows, lat), BF16),
            pltpu.SemaphoreType.DMA,
        ],
        compiler_params=params(),
        name="rim",
    )(*near_by(mix, east, north, fwd, near, got), away(bwd))
    far_w = lax.ppermute(own_e, "tile", ring)
    far_e = lax.ppermute(own_w, "tile", back)
    inner = pl.pallas_call(
        functools.partial(forcing_inner_kernel, lat=lat),
        in_specs=[here] * 3,
        out_specs=here,
        out_shape=pltpu.VMEM((total, inner_width), BF16),
        scratch_shapes=[ranges, pltpu.VMEM((total, cells), F32)],
        compiler_params=params(),
        name="forcing_inner",
    )(*near_by(weighted, place, middle))

    out = pl.pallas_call(
        functools.partial(second_half_kernel, lon=lon, levels=levels),
        in_specs=[here] * 8,
        out_specs=far,
        out_shape=jax.ShapeDtypeStruct((total * lon, lat), F32),
        scratch_shapes=scratch(lon + 2 * HALO, TOGETHER)
        + [pltpu.VMEM((total * lon, lat), F32), pltpu.SemaphoreType.DMA((steps,))],
        compiler_params=params(),
        name="second_half",
    )(*near_by(mix, inner_coef, rim_coef, far_w, own_w, inner, own_e, far_e))
    return out.reshape(tracers, levels, lon, lat)


def solution(mesh):
    in_specs = (
        P("ens", None, "tile", None),
        P("ens", "tile", None),
        P("ens", "tile", None),
        P(),
        P("ens", "tile"),
        P("ens", "tile"),
        P("tile", "ens"),
        P("ens", "tile"),
    )
    out_specs = P("ens", None, "tile", None)
    return jax.shard_map(
        per_device, mesh=mesh, in_specs=in_specs, out_specs=out_specs, check_vma=False
    )
```

```python
import functools

import jax
import jax.numpy as jnp
from jax import lax
from jax.experimental import pallas as pl
from jax.experimental.pallas import tpu as pltpu
from jax.sharding import PartitionSpec as P

F32 = jnp.float32
BF16 = jnp.bfloat16
GROUP = 2
RIM_TOGETHER = 4
TOGETHER = 2
HALO = 2
VMEM_BYTES = 20 * 1024 * 1024
VMEM = pltpu.MemorySpace.VMEM


def params(**more):
    return pltpu.CompilerParams(vmem_limit_bytes=VMEM_BYTES, **more)


def near_by(*arrays):
    return [pltpu.with_memory_space_constraint(array, VMEM) for array in arrays]


def away(array):
    return pltpu.with_memory_space_constraint(array, pltpu.MemorySpace.HBM)


def nt_dot(a, b):
    return lax.dot_general(a, b, (((1,), (1,)), ((), ())), preferred_element_type=F32)


def rows16(row):
    return jnp.broadcast_to(row, (16, row.shape[1])).astype(BF16)


def stacked(block, count):
    return jnp.concatenate([block] * count, axis=0)


def pack_kernel(
    owner_ref, column_ref, kernel_hbm, weight_hbm, out_hbm, kernel_ref, weight_ref, out_ref,
    in_sems, out_sems, *, tiles, capacity, lat, pairs,
):
    levels, pixels = kernel_ref.shape
    entering = [
        pltpu.make_async_copy(kernel_hbm, kernel_ref, in_sems.at[0]),
        pltpu.make_async_copy(weight_hbm, weight_ref, in_sems.at[1]),
    ]
    for copy in entering:
        copy.start()
    column = column_ref[...]
    longitude = column // lat
    line = lax.broadcasted_iota(jnp.int32, (8, pixels), 0)
    place = jnp.where(
        line == 0,
        (longitude + 1).astype(F32),
        jnp.where(line == 1, (column % lat).astype(F32), 0.0),
    )
    classes = tiles * pairs
    named = owner_ref[...] * pairs + longitude // HALO
    block = min(256, pixels)

    def iota(shape, dim):
        return lax.broadcasted_iota(jnp.int32, shape, dim)

    def flags(mask):
        return mask.astype(F32).astype(BF16)

    upto = flags(iota((block, block), 0) <= iota((block, block), 1))
    carry = jnp.zeros((classes, 1), F32)
    members, counted = [], []
    for start in range(0, pixels, block):
        member = named[:, start : start + block] == iota((classes, block), 0)
        counts = jnp.dot(flags(member), upto, preferred_element_type=F32) + carry
        carry = counts[:, block - 1 : block]
        members.append(member)
        counted.append(counts)
    size = jnp.broadcast_to(carry, (classes, 128))
    row, other = iota((classes, classes), 0), iota((classes, classes), 1)
    same = row // pairs == other // pairs
    sizes = size.astype(BF16)
    before = jnp.dot(flags(same & (other < row)), sizes, preferred_element_type=F32)
    after = jnp.dot(flags(same & (other >= row)), sizes, preferred_element_type=F32)
    pair = iota((classes, 128), 0) % pairs
    slack = pair.astype(F32) * (capacity // pairs) - before
    shift = 1
    while shift < pairs:
        slack = jnp.where(pair >= shift, jnp.maximum(slack, pltpu.roll(slack, shift, 0)), slack)
        shift = 2 * shift
    begin = jnp.minimum(before + slack, capacity - after)[:, :1]
    gather = flags(iota((tiles, classes), 0) == iota((tiles, classes), 1) // pairs)
    ranks = [
        jnp.dot(
            gather,
            jnp.where(member, begin + counts, 0.0).astype(BF16),
            preferred_element_type=F32,
        )
        - 1.0
        for member, counts in zip(members, counted)
    ]
    ranks = jnp.concatenate(ranks, axis=1)
    slot = iota((capacity, pixels), 0).astype(F32).astype(BF16)
    for copy in entering:
        copy.wait()
    payload = jnp.concatenate(
        [kernel_ref[...].astype(F32), weight_ref[...].astype(F32), place], axis=0
    ).astype(BF16)
    leaving = []
    for tile in range(tiles):
        rank = stacked(rows16(ranks[tile : tile + 1, :]), capacity // 16)
        chosen = jnp.where(slot == rank, jnp.ones_like(slot), jnp.zeros_like(slot))
        out_ref[tile] = nt_dot(payload, chosen).astype(BF16)
        copy = pltpu.make_async_copy(out_ref.at[tile], out_hbm.at[tile], out_sems.at[tile])
        copy.start()
        leaving.append(copy)
    for copy in leaving:
        copy.wait()


def both(ref, block, x, lon, levels):
    parts = [
        ref[pl.ds((t * levels + block * 8) * lon + x, 8, stride=lon), :] for t in range(GROUP)
    ]
    return jnp.concatenate(parts, axis=0).astype(BF16)


def edge_kernel(
    field_ref, east_ref, north_ref, level_mix_ref, fwd_ref, bwd_ref, mix_ref, *, lon, levels
):
    rows = GROUP * levels
    total = field_ref.shape[0] // lon
    for group in range(total // rows):
        view = field_ref.at[group * rows * lon : (group + 1) * rows * lon, :]
        for c in range(HALO):
            for block in range(levels // 8):
                spot = c * total + group * rows + block * 8 * GROUP
                at = slice(spot, spot + 8 * GROUP)
                fwd_ref[at, :] = both(view, block, lon - HALO + c, lon, levels)
                bwd_ref[at, :] = both(view, block, c, lon, levels)

    def put(out, place, ref, x):
        spot = HALO * total + place * (levels + 8)
        value = ref[pl.ds(x, levels, stride=lon), :]
        value = jnp.concatenate([value, jnp.zeros((8, value.shape[1]), F32)], axis=0)
        out[spot : spot + levels + 8, :] = value.astype(BF16)

    put(fwd_ref, 0, east_ref, lon - 2)
    put(fwd_ref, 1, east_ref, lon - 1)
    put(fwd_ref, 2, north_ref, lon - 1)
    put(bwd_ref, 0, east_ref, 0)
    put(bwd_ref, 1, north_ref, 0)
    row = lax.broadcasted_iota(jnp.int32, (rows, levels), 0)
    level = row // (8 * GROUP) * 8 + row % 8
    mine = level == lax.broadcasted_iota(jnp.int32, (rows, levels), 1)
    mix = jnp.zeros((rows, rows), F32)
    for t in range(GROUP):
        pick = (mine & (row // 8 % GROUP == t)).astype(F32).astype(BF16)
        mix = mix + nt_dot(nt_dot(pick, level_mix_ref[...]).astype(BF16), pick)
    mix_ref[...] = mix.astype(BF16)


def fill_coefs(east_ref, north_ref, edges, coef_ref, columns, lon, levels, total):
    lat = east_ref.shape[1]
    base = HALO * total

    def far(ref, place):
        spot = base + place * (levels + 8)
        return ref[spot : spot + levels + 8, :].astype(F32)[:levels]

    def own(ref, x):
        return ref[pl.ds(x, levels, stride=lon), :]

    def east(x):
        if x < 0:
            return far(edges[0], x + HALO)
        return own(east_ref, x) if x < lon else far(edges[1], 0)

    def north(x):
        if x < 0:
            return far(edges[0], 2)
        return own(north_ref, x) if x < lon else far(edges[1], 1)

    lane = lax.broadcasted_iota(jnp.int32, (levels, lat), 1)
    for i, x in enumerate(columns):
        at = slice(i * lat, (i + 1) * lat)
        face = jnp.where(lane < lat - 1, north(x), 0.0)
        to_east = jnp.maximum(east(x), 0.0)
        to_west = jnp.minimum(east(x - 1), 0.0)
        to_north = jnp.maximum(face, 0.0)
        to_south = pltpu.roll(jnp.minimum(face, 0.0), 1, 1)
        coef_ref[0, :, at] = (1.0 - to_east) + to_west + (to_south - to_north)
        coef_ref[1, :, at] = to_east
        coef_ref[2, :, at] = -to_west
        coef_ref[3, :, at] = to_north
        coef_ref[4, :, at] = -to_south


def stencil(mixed_ref, coef, start, count, lat, levels, emit):
    def column(e):
        return slice(e * lat, (e + 1) * lat)

    for block in range(levels // 8):
        lines = slice(block * 8, block * 8 + 8)
        tracer_rows = [
            slice(block * 8 * GROUP + 8 * t, block * 8 * GROUP + 8 * t + 8) for t in range(GROUP)
        ]
        left = [mixed_ref[r, column(start - 1)] for r in tracer_rows]
        centre = [mixed_ref[r, column(start)] for r in tracer_rows]
        for e in range(start, start + count):
            factor = [coef(j, lines, e) for j in range(5)]
            values = []
            for t, r in enumerate(tracer_rows):
                right = mixed_ref[r, column(e + 1)]
                value = (factor[0] * centre[t] + factor[1] * right) + (
                    factor[2] * left[t] + factor[3] * pltpu.roll(centre[t], lat - 1, 1)
                )
                values.append(value + factor[4] * pltpu.roll(centre[t], 1, 1))
                left[t], centre[t] = centre[t], right
            emit(block, e, values)


def two_steps(mix_ref, levels, lat, segments):
    def mix(field_ref, mixed_ref, lo, hi):
        for e in range(lo, hi, 2):
            at = slice(e * lat, (e + 2) * lat)
            mixed_ref[:, at] = jnp.dot(mix_ref[...], field_ref[:, at], preferred_element_type=F32)

    for field_ref, mixed_ref, _, start, count, _ in segments:
        mix(field_ref, mixed_ref, start, start + count)
    for field_ref, mixed_ref, coef, start, count, _ in segments:

        def keep(block, e, values):
            at = slice(block * 8 * GROUP, (block + 1) * 8 * GROUP)
            field_ref[at, e * lat : (e + 1) * lat] = jnp.concatenate(values, axis=0).astype(BF16)

        stencil(mixed_ref, coef, start + 1, count - 2, lat, levels, keep)
    for field_ref, mixed_ref, _, start, count, _ in segments:
        mix(field_ref, mixed_ref, start + 1, start + count - 1)
    for field_ref, mixed_ref, coef, start, count, put in segments:
        stencil(mixed_ref, coef, start + 2, count - 4, lat, levels, put)


def factors(coef_ref, lat, place_of):
    def coef(j, lines, e):
        place = place_of(e)
        return coef_ref[j, lines, place * lat : (place + 1) * lat]

    return coef


def inner_kernel(
    mix_ref, east_ref, north_ref, in_ref, out_ref, near_ref, coef_hbm, coef_ref, field_ref,
    mixed_ref, coef_sem, *, lon, levels,
):
    lat = in_ref.shape[1]
    rows = GROUP * levels
    step = pl.program_id(0)
    base = pl.multiple_of(step * rows * lon, 16)
    source = in_ref.at[pl.ds(base, rows * lon), :]

    @pl.when(step == 0)
    def _():
        fill_coefs(east_ref, north_ref, None, coef_ref, range(1, lon - 1), lon, levels, 0)
        pltpu.make_async_copy(coef_ref, coef_hbm, coef_sem).start()

    for x in range(lon):
        for block in range(levels // 8):
            at = slice(block * 8 * GROUP, (block + 1) * 8 * GROUP)
            field_ref[at, x * lat : (x + 1) * lat] = both(source, block, x, lon, levels)
    side = 2 * HALO * lat
    mine = pl.ds(pl.multiple_of(step * rows, 16), rows)
    near_ref[mine, :side] = field_ref[:, :side]
    near_ref[mine, side:] = field_ref[:, lon * lat - side :]

    def put(block, e, values):
        for t, value in enumerate(values):
            row = block * 8 * GROUP + 8 * t
            out_ref[row : row + 8, (e - HALO) * lat : (e - HALO + 1) * lat] = value

    coef = factors(coef_ref, lat, lambda e: e - 1)
    two_steps(mix_ref, levels, lat, [(field_ref, mixed_ref, coef, 0, lon, put)])

    @pl.when(step == pl.num_programs(0) - 1)
    def _():
        pltpu.make_async_copy(coef_ref, coef_hbm, coef_sem).wait()


def rim_kernel(
    mix_ref, east_ref, north_ref, fwd_ref, near_ref, got_ref, bwd_hbm, west_out_ref, east_out_ref,
    coef_ref, weighted_ref, place_ref, field_ref, mixed_ref, range_ref, total_ref, bwd_ref, bwd_sem,
    *, lon, levels, tracers,
):
    copy = pltpu.make_async_copy(bwd_hbm, bwd_ref, bwd_sem)
    copy.start()
    total = near_ref.shape[0]
    lat = fwd_ref.shape[1]
    rows = GROUP * levels
    wide = 3 * HALO
    weigh(got_ref, weighted_ref, place_ref, range_ref, lat, levels, tracers)
    copy.wait()
    columns = list(range(1 - HALO, HALO + 1)) + list(range(lon - HALO - 1, lon + HALO - 1))
    fill_coefs(east_ref, north_ref, (fwd_ref, bwd_ref), coef_ref, columns, lon, levels, total)
    together = field_ref.shape[0]

    def segment(group, slot, half):
        field, mixed = field_ref.at[slot], mixed_ref.at[slot]
        start = half * wide

        def put(block, e, values):
            spot = (e - start - HALO + half * HALO) * lat
            for t, value in enumerate(values):
                row = pl.multiple_of(group * rows + block * 8 * GROUP + 8 * t, 8)
                total_ref[pl.ds(row, 8), spot : spot + lat] = value

        coef = factors(coef_ref, lat, lambda e: e - start - 1 + half * 2 * HALO)
        return field, mixed, coef, start, wide, put

    def groups_of(i, carry):
        segments = []
        for slot in range(together):
            group = i * together + slot
            for c in range(HALO):
                at = pl.ds(pl.multiple_of(c * total + group * rows, 16), rows)
                field_ref[slot, :, c * lat : (c + 1) * lat] = fwd_ref[at, :]
                e = wide + 2 * HALO + c
                field_ref[slot, :, e * lat : (e + 1) * lat] = bwd_ref[at, :]
            side = 2 * HALO * lat
            mine = pl.ds(pl.multiple_of(group * rows, 16), rows)
            field_ref[slot, :, HALO * lat : HALO * lat + side] = near_ref[mine, :side]
            field_ref[slot, :, wide * lat : wide * lat + side] = near_ref[mine, side:]
            segments = segments + [segment(group, slot, half) for half in range(2)]
        two_steps(mix_ref, levels, lat, segments)
        return carry

    lax.fori_loop(0, total // rows // together, groups_of, 0)
    cells = HALO * lat
    for side, out_ref in ((0, west_out_ref), (1, east_out_ref)):
        at = slice(side * cells, (side + 1) * cells)
        pair = side * (lon // HALO - 1)
        add_forcing(weighted_ref, place_ref, range_ref, total_ref, at, float(pair * cells))
        out_ref[...] = total_ref[:, at].astype(BF16)


def second_half_kernel(
    mix_ref, inner_coef_ref, rim_coef_ref, far_w_ref, own_w_ref, inner_ref, own_e_ref, far_e_ref,
    out_hbm, field_ref, mixed_ref, result_ref, out_sems, *, lon, levels,
):
    lat = out_hbm.shape[1]
    rows = GROUP * levels
    groups = far_w_ref.shape[0] // rows

    def coef(j, lines, e):
        x = e - HALO
        if x < 1:
            ref, place = rim_coef_ref, x + HALO - 1
        elif x < lon - 1:
            ref, place = inner_coef_ref, x - 1
        else:
            ref, place = rim_coef_ref, x - (lon - HALO - 1) + 2 * HALO
        return ref[j, lines, place * lat : (place + 1) * lat]

    def leave(group):
        at = pl.ds(pl.multiple_of(group * rows * lon, 16), rows * lon)
        return pltpu.make_async_copy(result_ref.at[at, :], out_hbm.at[at, :], out_sems.at[group])

    together = field_ref.shape[0]

    def segment(group, slot):
        field = field_ref.at[slot]
        mine = pl.ds(pl.multiple_of(group * rows, 16), rows)
        spot = 0
        for ref in (far_w_ref, own_w_ref, inner_ref, own_e_ref, far_e_ref):
            width = ref.shape[1]
            field[:, spot : spot + width] = ref[mine, :]
            spot = spot + width
        base = pl.multiple_of(group * rows * lon, 16)
        result = result_ref.at[pl.ds(base, rows * lon), :]

        def put(block, e, values):
            for t, value in enumerate(values):
                first = (t * levels + block * 8) * lon + e - HALO
                result[pl.ds(first, 8, stride=lon), :] = value

        return field, mixed_ref.at[slot], coef, 0, lon + 2 * HALO, put

    def groups_of(i, carry):
        mine = [i * together + slot for slot in range(together)]
        two_steps(mix_ref, levels, lat, [segment(group, slot) for slot, group in enumerate(mine)])
        for group in mine:
            leave(group).start()
        return carry

    lax.fori_loop(0, groups // together, groups_of, 0)
    for group in range(groups):
        leave(group).wait()


def regions_of(capacity):
    return capacity // 64 if capacity % 128 == 0 else 1


def regroup(got_ref, store):
    tiles, height, capacity = got_ref.shape
    if regions_of(capacity) == 1:
        for tile in range(tiles):
            store(tile * capacity, got_ref[tile].astype(F32))
        return
    low = lax.broadcasted_iota(jnp.int32, (height, 128), 1) < 64
    for tile in range(0, tiles, 2):
        for half in range(capacity // 128):
            at = slice(half * 128, half * 128 + 128)
            one, two = got_ref[tile, :, at].astype(F32), got_ref[tile + 1, :, at].astype(F32)
            spot = 2 * half * tiles * 64 + tile * 64
            store(spot, jnp.where(low, one, pltpu.roll(two, 64, 1)))
            store(spot + tiles * 64, jnp.where(low, pltpu.roll(one, 64, 1), two))


def weigh(got_ref, weighted_ref, place_ref, range_ref, lat, levels, tracers):
    def store(spot, got):
        at = slice(spot, spot + got.shape[1])
        row = 0
        for t in range(0, tracers, GROUP):
            for block in range(0, levels, 8):
                kernel = got[block : block + 8]
                pieces = [
                    kernel * got[levels + j : levels + j + 1, :] for j in range(t, t + GROUP)
                ]
                value = jnp.concatenate(pieces, axis=0).astype(BF16)
                weighted_ref[row : row + 8 * GROUP, at] = value
                row = row + 8 * GROUP
        first = levels + tracers
        column = (got[first : first + 1, :] - 1.0) * lat + got[first + 1 : first + 2, :]
        place_ref[:, at] = jnp.broadcast_to(column, (8, got.shape[1]))

    regroup(got_ref, store)
    span(place_ref, range_ref)


def span(place_ref, range_ref):
    parts = range_ref.shape[0] // 2
    wide = place_ref.shape[1] // parts
    for part in range(parts):
        place = place_ref[:, part * wide : (part + 1) * wide]
        range_ref[2 * part] = jnp.min(jnp.where(place < 0.0, 1e6, place))
        range_ref[2 * part + 1] = jnp.max(place)


def add_forcing(weighted_ref, place_ref, range_ref, total_ref, columns, offset):
    cells = total_ref[:, columns].shape[1]
    parts = range_ref.shape[0] // 2
    wide = weighted_ref.shape[1] // parts
    for part in range(parts):
        held = (range_ref[2 * part] < offset + cells) & (range_ref[2 * part + 1] >= offset)

        @pl.when(held)
        def _():
            at = slice(part * wide, (part + 1) * wide)
            key = rows16(place_ref[0:1, at] - offset)
            cell = lax.broadcasted_iota(jnp.int32, (cells, wide), 0).astype(F32).astype(BF16)
            hit = cell == stacked(key, cells // 16)
            one_hot = jnp.where(hit, jnp.ones_like(cell), jnp.zeros_like(cell))
            total_ref[:, columns] += nt_dot(weighted_ref[:, at], one_hot)


def forcing_inner_kernel(
    weighted_ref, place_ref, field_ref, out_ref, range_ref, total_ref, *, lat
):
    cells = HALO * lat
    span(place_ref, range_ref)

    def pair_of(i, carry):
        at = pl.ds(pl.multiple_of(i * cells, cells), cells)
        total_ref[...] = field_ref[:, at]
        offset = ((i + 1) * cells).astype(F32)
        add_forcing(weighted_ref, place_ref, range_ref, total_ref, slice(0, cells), offset)
        out_ref[:, at] = total_ref[...].astype(BF16)
        return carry

    lax.fori_loop(0, field_ref.shape[1] // cells, pair_of, 0)


def per_device(
    adjoint_in,
    east_courant,
    north_courant,
    level_mix,
    avg_kernel,
    pixel_weight,
    pixel_owner,
    pixel_column,
):
    tracers, levels, lon, lat = adjoint_in.shape
    pixels = avg_kernel.shape[1]
    tiles = lax.axis_size("tile")
    capacity = 4 * pixels // tiles
    slots = tiles * capacity
    total = tracers * levels
    steps = tracers // GROUP
    rows = GROUP * levels
    ring = [(i, (i + 1) % tiles) for i in range(tiles)]
    back = [((i + 1) % tiles, i) for i in range(tiles)]

    field = adjoint_in.reshape(total * lon, lat)
    east = east_courant.reshape(levels * lon, lat)
    north = north_courant.reshape(levels * lon, lat)
    here = pl.BlockSpec(memory_space=VMEM)
    far = pl.BlockSpec(memory_space=pltpu.MemorySpace.HBM)
    pairs = lon // HALO
    height = levels + tracers + 8
    payload = pl.pallas_call(
        functools.partial(pack_kernel, tiles=tiles, capacity=capacity, lat=lat, pairs=pairs),
        in_specs=[pl.BlockSpec((1, pixels), lambda: (0, 0))] * 2 + [far] * 2,
        out_specs=far,
        out_shape=pltpu.HBM((tiles, height, capacity), BF16),
        scratch_shapes=[
            pltpu.VMEM((levels, pixels), BF16),
            pltpu.VMEM((tracers, pixels), BF16),
            pltpu.VMEM((tiles, height, capacity), BF16),
            pltpu.SemaphoreType.DMA((2,)),
            pltpu.SemaphoreType.DMA((tiles,)),
        ],
        compiler_params=params(),
        name="pack",
    )(
        away(pixel_owner.reshape(1, pixels)),
        away(pixel_column),
        away(avg_kernel),
        away(pixel_weight),
    )
    got = lax.all_to_all(payload, "tile", split_axis=0, concat_axis=0, tiled=True)

    fwd_rows = HALO * total + 3 * (levels + 8)
    bwd_rows = HALO * total + 2 * (levels + 8)
    fwd, bwd, mix = pl.pallas_call(
        functools.partial(edge_kernel, lon=lon, levels=levels),
        in_specs=[here, here, here, pl.BlockSpec((levels, levels), lambda: (0, 0))],
        out_specs=[here] * 3,
        out_shape=[
            pltpu.VMEM((fwd_rows, lat), BF16),
            pltpu.VMEM((bwd_rows, lat), BF16),
            pltpu.VMEM((rows, rows), BF16),
        ],
        compiler_params=params(),
        name="edges",
    )(*near_by(field, east, north), away(level_mix))
    fwd = lax.ppermute(fwd, "tile", ring)
    bwd = lax.ppermute(bwd, "tile", back)

    def scratch(columns, *together):
        return [
            pltpu.VMEM((*together, rows, columns * lat), BF16),
            pltpu.VMEM((*together, rows, columns * lat), F32),
        ]

    cells = HALO * lat
    inner_width = (lon - 2 * HALO) * lat
    middle, near, inner_coef = pl.pallas_call(
        functools.partial(inner_kernel, lon=lon, levels=levels),
        grid=(steps,),
        in_specs=[here] * 4,
        out_specs=[pl.BlockSpec((rows, inner_width), lambda i: (i, 0)), here, far],
        out_shape=[
            pltpu.HBM((total, inner_width), F32),
            pltpu.VMEM((total, 4 * cells), BF16),
            pltpu.HBM((5, levels, (lon - 2) * lat), F32),
        ],
        scratch_shapes=[pltpu.VMEM((5, levels, (lon - 2) * lat), F32)]
        + scratch(lon)
        + [pltpu.SemaphoreType.DMA],
        compiler_params=params(),
        name="first_half_inner",
    )(*near_by(mix, east, north, field))

    ranges = pltpu.SMEM((2 * regions_of(capacity),), F32)
    own_w, own_e, rim_coef, weighted, place = pl.pallas_call(
        functools.partial(rim_kernel, lon=lon, levels=levels, tracers=tracers),
        in_specs=[here] * 6 + [far],
        out_specs=[here] * 5,
        out_shape=[
            pltpu.VMEM((total, cells), BF16),
            pltpu.VMEM((total, cells), BF16),
            pltpu.VMEM((5, levels, 4 * HALO * lat), F32),
            pltpu.VMEM((total, slots), BF16),
            pltpu.VMEM((8, slots), F32),
        ],
        scratch_shapes=scratch(6 * HALO, RIM_TOGETHER)
        + [
            ranges,
            pltpu.VMEM((total, 2 * cells), F32),
            pltpu.VMEM((bwd_rows, lat), BF16),
            pltpu.SemaphoreType.DMA,
        ],
        compiler_params=params(),
        name="rim",
    )(*near_by(mix, east, north, fwd, near, got), away(bwd))
    far_w = lax.ppermute(own_e, "tile", ring)
    far_e = lax.ppermute(own_w, "tile", back)
    inner = pl.pallas_call(
        functools.partial(forcing_inner_kernel, lat=lat),
        in_specs=[here] * 3,
        out_specs=here,
        out_shape=pltpu.VMEM((total, inner_width), BF16),
        scratch_shapes=[ranges, pltpu.VMEM((total, cells), F32)],
        compiler_params=params(),
        name="forcing_inner",
    )(*near_by(weighted, place, middle))

    out = pl.pallas_call(
        functools.partial(second_half_kernel, lon=lon, levels=levels),
        in_specs=[here] * 8,
        out_specs=far,
        out_shape=jax.ShapeDtypeStruct((total * lon, lat), F32),
        scratch_shapes=scratch(lon + 2 * HALO, TOGETHER)
        + [pltpu.VMEM((total * lon, lat), F32), pltpu.SemaphoreType.DMA((steps,))],
        compiler_params=params(),
        name="second_half",
    )(*near_by(mix, inner_coef, rim_coef, far_w, own_w, inner, own_e, far_e))
    return out.reshape(tracers, levels, lon, lat)


def solution(mesh):
    in_specs = (
        P("ens", None, "tile", None),
        P("ens", "tile", None),
        P("ens", "tile", None),
        P(),
        P("ens", "tile"),
        P("ens", "tile"),
        P("tile", "ens"),
        P("ens", "tile"),
    )
    out_specs = P("ens", None, "tile", None)
    return jax.shard_map(
        per_device, mesh=mesh, in_specs=in_specs, out_specs=out_specs, check_vma=False
    )
```

```python
import functools

import jax
import jax.numpy as jnp
from jax import lax
from jax.experimental import pallas as pl
from jax.experimental.pallas import tpu as pltpu
from jax.sharding import PartitionSpec as P

F32 = jnp.float32
BF16 = jnp.bfloat16
GROUP = 2
RIM_TOGETHER = 4
TOGETHER = 2
HALO = 2
VMEM_BYTES = 20 * 1024 * 1024
VMEM = pltpu.MemorySpace.VMEM


def params(**more):
    return pltpu.CompilerParams(vmem_limit_bytes=VMEM_BYTES, **more)


def near_by(*arrays):
    return [pltpu.with_memory_space_constraint(array, VMEM) for array in arrays]


def away(array):
    return pltpu.with_memory_space_constraint(array, pltpu.MemorySpace.HBM)


def nt_dot(a, b):
    return lax.dot_general(a, b, (((1,), (1,)), ((), ())), preferred_element_type=F32)


def rows16(row):
    return jnp.broadcast_to(row, (16, row.shape[1])).astype(BF16)


def stacked(block, count):
    return jnp.concatenate([block] * count, axis=0)


def pack_kernel(
    owner_ref, column_ref, kernel_hbm, weight_hbm, out_hbm, kernel_ref, weight_ref, out_ref,
    in_sems, out_sems, *, tiles, capacity, lat, pairs,
):
    levels, pixels = kernel_ref.shape
    entering = [
        pltpu.make_async_copy(kernel_hbm, kernel_ref, in_sems.at[0]),
        pltpu.make_async_copy(weight_hbm, weight_ref, in_sems.at[1]),
    ]
    for copy in entering:
        copy.start()
    column = column_ref[...]
    longitude = column // lat
    line = lax.broadcasted_iota(jnp.int32, (8, pixels), 0)
    place = jnp.where(
        line == 0,
        (longitude + 1).astype(F32),
        jnp.where(line == 1, (column % lat).astype(F32), 0.0),
    )
    classes = tiles * pairs
    named = owner_ref[...] * pairs + longitude // HALO
    block = min(256, pixels)

    def iota(shape, dim):
        return lax.broadcasted_iota(jnp.int32, shape, dim)

    def flags(mask):
        return mask.astype(F32).astype(BF16)

    upto = flags(iota((block, block), 0) <= iota((block, block), 1))
    carry = jnp.zeros((classes, 1), F32)
    members, counted = [], []
    for start in range(0, pixels, block):
        member = named[:, start : start + block] == iota((classes, block), 0)
        counts = jnp.dot(flags(member), upto, preferred_element_type=F32) + carry
        carry = counts[:, block - 1 : block]
        members.append(member)
        counted.append(counts)
    size = jnp.broadcast_to(carry, (classes, 128))
    row, other = iota((classes, classes), 0), iota((classes, classes), 1)
    same = row // pairs == other // pairs
    sizes = size.astype(BF16)
    before = jnp.dot(flags(same & (other < row)), sizes, preferred_element_type=F32)
    after = jnp.dot(flags(same & (other >= row)), sizes, preferred_element_type=F32)
    pair = iota((classes, 128), 0) % pairs
    slack = pair.astype(F32) * (capacity // pairs) - before
    shift = 1
    while shift < pairs:
        slack = jnp.where(pair >= shift, jnp.maximum(slack, pltpu.roll(slack, shift, 0)), slack)
        shift = 2 * shift
    begin = jnp.minimum(before + slack, capacity - after)[:, :1]
    gather = flags(iota((tiles, classes), 0) == iota((tiles, classes), 1) // pairs)
    ranks = [
        jnp.dot(
            gather,
            jnp.where(member, begin + counts, 0.0).astype(BF16),
            preferred_element_type=F32,
        )
        - 1.0
        for member, counts in zip(members, counted)
    ]
    ranks = jnp.concatenate(ranks, axis=1)
    slot = iota((capacity, pixels), 0).astype(F32).astype(BF16)
    for copy in entering:
        copy.wait()
    payload = jnp.concatenate(
        [kernel_ref[...].astype(F32), weight_ref[...].astype(F32), place], axis=0
    ).astype(BF16)
    leaving = []
    for tile in range(tiles):
        rank = stacked(rows16(ranks[tile : tile + 1, :]), capacity // 16)
        chosen = jnp.where(slot == rank, jnp.ones_like(slot), jnp.zeros_like(slot))
        out_ref[tile] = nt_dot(payload, chosen).astype(BF16)
        copy = pltpu.make_async_copy(out_ref.at[tile], out_hbm.at[tile], out_sems.at[tile])
        copy.start()
        leaving.append(copy)
    for copy in leaving:
        copy.wait()


def both(ref, block, x, lon, levels):
    parts = [
        ref[pl.ds((t * levels + block * 8) * lon + x, 8, stride=lon), :] for t in range(GROUP)
    ]
    return jnp.concatenate(parts, axis=0).astype(BF16)


def edge_kernel(
    field_ref, east_ref, north_ref, level_mix_ref, fwd_ref, bwd_ref, mix_ref, *, lon, levels
):
    rows = GROUP * levels
    total = field_ref.shape[0] // lon
    for group in range(total // rows):
        view = field_ref.at[group * rows * lon : (group + 1) * rows * lon, :]
        for c in range(HALO):
            for block in range(levels // 8):
                spot = c * total + group * rows + block * 8 * GROUP
                at = slice(spot, spot + 8 * GROUP)
                fwd_ref[at, :] = both(view, block, lon - HALO + c, lon, levels)
                bwd_ref[at, :] = both(view, block, c, lon, levels)

    def put(out, place, ref, x):
        spot = HALO * total + place * (levels + 8)
        value = ref[pl.ds(x, levels, stride=lon), :]
        value = jnp.concatenate([value, jnp.zeros((8, value.shape[1]), F32)], axis=0)
        out[spot : spot + levels + 8, :] = value.astype(BF16)

    put(fwd_ref, 0, east_ref, lon - 2)
    put(fwd_ref, 1, east_ref, lon - 1)
    put(fwd_ref, 2, north_ref, lon - 1)
    put(bwd_ref, 0, east_ref, 0)
    put(bwd_ref, 1, north_ref, 0)
    row = lax.broadcasted_iota(jnp.int32, (rows, levels), 0)
    level = row // (8 * GROUP) * 8 + row % 8
    mine = level == lax.broadcasted_iota(jnp.int32, (rows, levels), 1)
    mix = jnp.zeros((rows, rows), F32)
    for t in range(GROUP):
        pick = (mine & (row // 8 % GROUP == t)).astype(F32).astype(BF16)
        mix = mix + nt_dot(nt_dot(pick, level_mix_ref[...]).astype(BF16), pick)
    mix_ref[...] = mix.astype(BF16)


def fill_coefs(east_ref, north_ref, edges, coef_ref, columns, lon, levels, total):
    lat = east_ref.shape[1]
    base = HALO * total

    def far(ref, place):
        spot = base + place * (levels + 8)
        return ref[spot : spot + levels + 8, :].astype(F32)[:levels]

    def own(ref, x):
        return ref[pl.ds(x, levels, stride=lon), :]

    def east(x):
        if x < 0:
            return far(edges[0], x + HALO)
        return own(east_ref, x) if x < lon else far(edges[1], 0)

    def north(x):
        if x < 0:
            return far(edges[0], 2)
        return own(north_ref, x) if x < lon else far(edges[1], 1)

    lane = lax.broadcasted_iota(jnp.int32, (levels, lat), 1)
    for i, x in enumerate(columns):
        at = slice(i * lat, (i + 1) * lat)
        face = jnp.where(lane < lat - 1, north(x), 0.0)
        to_east = jnp.maximum(east(x), 0.0)
        to_west = jnp.minimum(east(x - 1), 0.0)
        to_north = jnp.maximum(face, 0.0)
        to_south = pltpu.roll(jnp.minimum(face, 0.0), 1, 1)
        coef_ref[0, :, at] = (1.0 - to_east) + to_west + (to_south - to_north)
        coef_ref[1, :, at] = to_east
        coef_ref[2, :, at] = -to_west
        coef_ref[3, :, at] = to_north
        coef_ref[4, :, at] = -to_south


def stencil(mixed_ref, coef, start, count, lat, levels, emit, after=None):
    def column(e):
        return slice(e * lat, (e + 1) * lat)

    for block in range(levels // 8):
        lines = slice(block * 8, block * 8 + 8)
        tracer_rows = [
            slice(block * 8 * GROUP + 8 * t, block * 8 * GROUP + 8 * t + 8) for t in range(GROUP)
        ]
        left = [mixed_ref[r, column(start - 1)] for r in tracer_rows]
        centre = [mixed_ref[r, column(start)] for r in tracer_rows]
        for e in range(start, start + count):
            factor = [coef(j, lines, e) for j in range(5)]
            values = []
            for t, r in enumerate(tracer_rows):
                right = mixed_ref[r, column(e + 1)]
                value = (factor[0] * centre[t] + factor[1] * right) + (
                    factor[2] * left[t] + factor[3] * pltpu.roll(centre[t], lat - 1, 1)
                )
                values.append(value + factor[4] * pltpu.roll(centre[t], 1, 1))
                left[t], centre[t] = centre[t], right
            emit(block, e, values)
        if after is not None:
            after(block)


def two_steps(mix_ref, levels, lat, segments, afters=None):
    def mix(field_ref, mixed_ref, lo, hi):
        for e in range(lo, hi, 2):
            at = slice(e * lat, (e + 2) * lat)
            mixed_ref[:, at] = jnp.dot(mix_ref[...], field_ref[:, at], preferred_element_type=F32)

    for field_ref, mixed_ref, _, start, count, _ in segments:
        mix(field_ref, mixed_ref, start, start + count)
    for field_ref, mixed_ref, coef, start, count, _ in segments:

        def keep(block, e, values):
            at = slice(block * 8 * GROUP, (block + 1) * 8 * GROUP)
            field_ref[at, e * lat : (e + 1) * lat] = jnp.concatenate(values, axis=0).astype(BF16)

        stencil(mixed_ref, coef, start + 1, count - 2, lat, levels, keep)
    for field_ref, mixed_ref, _, start, count, _ in segments:
        mix(field_ref, mixed_ref, start + 1, start + count - 1)
    for i, (field_ref, mixed_ref, coef, start, count, put) in enumerate(segments):
        after = afters[i] if afters else None
        stencil(mixed_ref, coef, start + 2, count - 4, lat, levels, put, after)


def factors(coef_ref, lat, place_of):
    def coef(j, lines, e):
        place = place_of(e)
        return coef_ref[j, lines, place * lat : (place + 1) * lat]

    return coef


def inner_kernel(
    mix_ref, east_ref, north_ref, in_ref, out_ref, near_ref, coef_hbm, coef_ref, field_ref,
    mixed_ref, coef_sem, *, lon, levels,
):
    lat = in_ref.shape[1]
    rows = GROUP * levels
    step = pl.program_id(0)
    base = pl.multiple_of(step * rows * lon, 16)
    source = in_ref.at[pl.ds(base, rows * lon), :]

    @pl.when(step == 0)
    def _():
        fill_coefs(east_ref, north_ref, None, coef_ref, range(1, lon - 1), lon, levels, 0)
        pltpu.make_async_copy(coef_ref, coef_hbm, coef_sem).start()

    for x in range(lon):
        for block in range(levels // 8):
            at = slice(block * 8 * GROUP, (block + 1) * 8 * GROUP)
            field_ref[at, x * lat : (x + 1) * lat] = both(source, block, x, lon, levels)
    side = 2 * HALO * lat
    mine = pl.ds(pl.multiple_of(step * rows, 16), rows)
    near_ref[mine, :side] = field_ref[:, :side]
    near_ref[mine, side:] = field_ref[:, lon * lat - side :]

    def put(block, e, values):
        for t, value in enumerate(values):
            row = block * 8 * GROUP + 8 * t
            out_ref[row : row + 8, (e - HALO) * lat : (e - HALO + 1) * lat] = value

    coef = factors(coef_ref, lat, lambda e: e - 1)
    two_steps(mix_ref, levels, lat, [(field_ref, mixed_ref, coef, 0, lon, put)])

    @pl.when(step == pl.num_programs(0) - 1)
    def _():
        pltpu.make_async_copy(coef_ref, coef_hbm, coef_sem).wait()


def rim_kernel(
    mix_ref, east_ref, north_ref, fwd_ref, near_ref, got_ref, bwd_hbm, west_out_ref, east_out_ref,
    coef_ref, weighted_ref, place_ref, field_ref, mixed_ref, range_ref, total_ref, bwd_ref, bwd_sem,
    *, lon, levels, tracers,
):
    copy = pltpu.make_async_copy(bwd_hbm, bwd_ref, bwd_sem)
    copy.start()
    total = near_ref.shape[0]
    lat = fwd_ref.shape[1]
    rows = GROUP * levels
    wide = 3 * HALO
    weigh(got_ref, weighted_ref, place_ref, range_ref, lat, levels, tracers)
    copy.wait()
    columns = list(range(1 - HALO, HALO + 1)) + list(range(lon - HALO - 1, lon + HALO - 1))
    fill_coefs(east_ref, north_ref, (fwd_ref, bwd_ref), coef_ref, columns, lon, levels, total)
    together = field_ref.shape[0]

    def segment(group, slot, half):
        field, mixed = field_ref.at[slot], mixed_ref.at[slot]
        start = half * wide

        def put(block, e, values):
            spot = (e - start - HALO + half * HALO) * lat
            for t, value in enumerate(values):
                row = pl.multiple_of(group * rows + block * 8 * GROUP + 8 * t, 8)
                total_ref[pl.ds(row, 8), spot : spot + lat] = value

        coef = factors(coef_ref, lat, lambda e: e - start - 1 + half * 2 * HALO)
        return field, mixed, coef, start, wide, put

    def groups_of(i, carry):
        segments = []
        for slot in range(together):
            group = i * together + slot
            for c in range(HALO):
                at = pl.ds(pl.multiple_of(c * total + group * rows, 16), rows)
                field_ref[slot, :, c * lat : (c + 1) * lat] = fwd_ref[at, :]
                e = wide + 2 * HALO + c
                field_ref[slot, :, e * lat : (e + 1) * lat] = bwd_ref[at, :]
            side = 2 * HALO * lat
            mine = pl.ds(pl.multiple_of(group * rows, 16), rows)
            field_ref[slot, :, HALO * lat : HALO * lat + side] = near_ref[mine, :side]
            field_ref[slot, :, wide * lat : wide * lat + side] = near_ref[mine, side:]
            segments = segments + [segment(group, slot, half) for half in range(2)]
        two_steps(mix_ref, levels, lat, segments)
        return carry

    lax.fori_loop(0, total // rows // together, groups_of, 0)
    cells = HALO * lat
    for side, out_ref in ((0, west_out_ref), (1, east_out_ref)):
        at = slice(side * cells, (side + 1) * cells)
        pair = side * (lon // HALO - 1)
        add_forcing(weighted_ref, place_ref, range_ref, total_ref, at, float(pair * cells))
        out_ref[...] = total_ref[:, at].astype(BF16)


def second_half_kernel(
    mix_ref, inner_coef_ref, rim_coef_ref, far_w_ref, own_w_ref, inner_ref, own_e_ref, far_e_ref,
    out_hbm, field_ref, mixed_ref, result_ref, out_sems, *, lon, levels,
):
    lat = out_hbm.shape[1]
    rows = GROUP * levels
    groups = far_w_ref.shape[0] // rows

    def coef(j, lines, e):
        x = e - HALO
        if x < 1:
            ref, place = rim_coef_ref, x + HALO - 1
        elif x < lon - 1:
            ref, place = inner_coef_ref, x - 1
        else:
            ref, place = rim_coef_ref, x - (lon - HALO - 1) + 2 * HALO
        return ref[j, lines, place * lat : (place + 1) * lat]

    blocks = levels // 8
    chunk = 3 if blocks % 3 == 0 else blocks
    size = chunk * 8 * lon

    def leave(group, part):
        copies = []
        for t in range(GROUP):
            first = group * rows * lon + t * levels * lon + part * size
            at = pl.ds(pl.multiple_of(first, 16), size)
            copies.append(
                pltpu.make_async_copy(
                    result_ref.at[at, :], out_hbm.at[at, :], out_sems.at[group, part, t]
                )
            )
        return copies

    together = field_ref.shape[0]

    def segment(group, slot):
        field = field_ref.at[slot]
        mine = pl.ds(pl.multiple_of(group * rows, 16), rows)
        spot = 0
        for ref in (far_w_ref, own_w_ref, inner_ref, own_e_ref, far_e_ref):
            width = ref.shape[1]
            field[:, spot : spot + width] = ref[mine, :]
            spot = spot + width
        base = pl.multiple_of(group * rows * lon, 16)
        result = result_ref.at[pl.ds(base, rows * lon), :]

        def put(block, e, values):
            for t, value in enumerate(values):
                first = (t * levels + block * 8) * lon + e - HALO
                result[pl.ds(first, 8, stride=lon), :] = value

        return field, mixed_ref.at[slot], coef, 0, lon + 2 * HALO, put

    def groups_of(i, carry):
        mine = [i * together + slot for slot in range(together)]

        def leaver(group):
            def after(block):
                if (block + 1) % chunk == 0:
                    for copy in leave(group, block // chunk):
                        copy.start()

            return after

        segments = [segment(group, slot) for slot, group in enumerate(mine)]
        two_steps(mix_ref, levels, lat, segments, [leaver(group) for group in mine])
        return carry

    lax.fori_loop(0, groups // together, groups_of, 0)
    for group in range(groups):
        for part in range(blocks // chunk):
            for copy in leave(group, part):
                copy.wait()


def regions_of(capacity):
    return capacity // 64 if capacity % 128 == 0 else 1


def regroup(got_ref, store):
    tiles, height, capacity = got_ref.shape
    if regions_of(capacity) == 1:
        for tile in range(tiles):
            store(tile * capacity, got_ref[tile].astype(F32))
        return
    low = lax.broadcasted_iota(jnp.int32, (height, 128), 1) < 64
    for tile in range(0, tiles, 2):
        for half in range(capacity // 128):
            at = slice(half * 128, half * 128 + 128)
            one, two = got_ref[tile, :, at].astype(F32), got_ref[tile + 1, :, at].astype(F32)
            spot = 2 * half * tiles * 64 + tile * 64
            store(spot, jnp.where(low, one, pltpu.roll(two, 64, 1)))
            store(spot + tiles * 64, jnp.where(low, pltpu.roll(one, 64, 1), two))


def weigh(got_ref, weighted_ref, place_ref, range_ref, lat, levels, tracers):
    def store(spot, got):
        at = slice(spot, spot + got.shape[1])
        row = 0
        for t in range(0, tracers, GROUP):
            for block in range(0, levels, 8):
                kernel = got[block : block + 8]
                pieces = [
                    kernel * got[levels + j : levels + j + 1, :] for j in range(t, t + GROUP)
                ]
                value = jnp.concatenate(pieces, axis=0).astype(BF16)
                weighted_ref[row : row + 8 * GROUP, at] = value
                row = row + 8 * GROUP
        first = levels + tracers
        column = (got[first : first + 1, :] - 1.0) * lat + got[first + 1 : first + 2, :]
        place_ref[:, at] = jnp.broadcast_to(column, (8, got.shape[1]))

    regroup(got_ref, store)
    span(place_ref, range_ref)


def span(place_ref, range_ref):
    parts = range_ref.shape[0] // 2
    wide = place_ref.shape[1] // parts
    for part in range(parts):
        place = place_ref[:, part * wide : (part + 1) * wide]
        range_ref[2 * part] = jnp.min(jnp.where(place < 0.0, 1e6, place))
        range_ref[2 * part + 1] = jnp.max(place)


def add_forcing(weighted_ref, place_ref, range_ref, total_ref, columns, offset):
    cells = total_ref[:, columns].shape[1]
    parts = range_ref.shape[0] // 2
    wide = weighted_ref.shape[1] // parts
    for part in range(parts):
        held = (range_ref[2 * part] < offset + cells) & (range_ref[2 * part + 1] >= offset)

        @pl.when(held)
        def _():
            at = slice(part * wide, (part + 1) * wide)
            key = rows16(place_ref[0:1, at] - offset)
            cell = lax.broadcasted_iota(jnp.int32, (cells, wide), 0).astype(F32).astype(BF16)
            hit = cell == stacked(key, cells // 16)
            one_hot = jnp.where(hit, jnp.ones_like(cell), jnp.zeros_like(cell))
            total_ref[:, columns] += nt_dot(weighted_ref[:, at], one_hot)


def forcing_inner_kernel(
    weighted_ref, place_ref, field_ref, out_ref, range_ref, total_ref, *, lat
):
    cells = HALO * lat
    span(place_ref, range_ref)

    def pair_of(i, carry):
        at = pl.ds(pl.multiple_of(i * cells, cells), cells)
        total_ref[...] = field_ref[:, at]
        offset = ((i + 1) * cells).astype(F32)
        add_forcing(weighted_ref, place_ref, range_ref, total_ref, slice(0, cells), offset)
        out_ref[:, at] = total_ref[...].astype(BF16)
        return carry

    lax.fori_loop(0, field_ref.shape[1] // cells, pair_of, 0)


def per_device(
    adjoint_in,
    east_courant,
    north_courant,
    level_mix,
    avg_kernel,
    pixel_weight,
    pixel_owner,
    pixel_column,
):
    tracers, levels, lon, lat = adjoint_in.shape
    pixels = avg_kernel.shape[1]
    tiles = lax.axis_size("tile")
    capacity = 4 * pixels // tiles
    slots = tiles * capacity
    total = tracers * levels
    steps = tracers // GROUP
    rows = GROUP * levels
    ring = [(i, (i + 1) % tiles) for i in range(tiles)]
    back = [((i + 1) % tiles, i) for i in range(tiles)]

    field = adjoint_in.reshape(total * lon, lat)
    east = east_courant.reshape(levels * lon, lat)
    north = north_courant.reshape(levels * lon, lat)
    here = pl.BlockSpec(memory_space=VMEM)
    far = pl.BlockSpec(memory_space=pltpu.MemorySpace.HBM)
    pairs = lon // HALO
    height = levels + tracers + 8
    payload = pl.pallas_call(
        functools.partial(pack_kernel, tiles=tiles, capacity=capacity, lat=lat, pairs=pairs),
        in_specs=[pl.BlockSpec((1, pixels), lambda: (0, 0))] * 2 + [far] * 2,
        out_specs=far,
        out_shape=pltpu.HBM((tiles, height, capacity), BF16),
        scratch_shapes=[
            pltpu.VMEM((levels, pixels), BF16),
            pltpu.VMEM((tracers, pixels), BF16),
            pltpu.VMEM((tiles, height, capacity), BF16),
            pltpu.SemaphoreType.DMA((2,)),
            pltpu.SemaphoreType.DMA((tiles,)),
        ],
        compiler_params=params(),
        name="pack",
    )(
        away(pixel_owner.reshape(1, pixels)),
        away(pixel_column),
        away(avg_kernel),
        away(pixel_weight),
    )
    got = lax.all_to_all(payload, "tile", split_axis=0, concat_axis=0, tiled=True)

    fwd_rows = HALO * total + 3 * (levels + 8)
    bwd_rows = HALO * total + 2 * (levels + 8)
    fwd, bwd, mix = pl.pallas_call(
        functools.partial(edge_kernel, lon=lon, levels=levels),
        in_specs=[here, here, here, pl.BlockSpec((levels, levels), lambda: (0, 0))],
        out_specs=[here] * 3,
        out_shape=[
            pltpu.VMEM((fwd_rows, lat), BF16),
            pltpu.VMEM((bwd_rows, lat), BF16),
            pltpu.VMEM((rows, rows), BF16),
        ],
        compiler_params=params(),
        name="edges",
    )(*near_by(field, east, north), away(level_mix))
    fwd = lax.ppermute(fwd, "tile", ring)
    bwd = lax.ppermute(bwd, "tile", back)

    def scratch(columns, *together):
        return [
            pltpu.VMEM((*together, rows, columns * lat), BF16),
            pltpu.VMEM((*together, rows, columns * lat), F32),
        ]

    cells = HALO * lat
    inner_width = (lon - 2 * HALO) * lat
    middle, near, inner_coef = pl.pallas_call(
        functools.partial(inner_kernel, lon=lon, levels=levels),
        grid=(steps,),
        in_specs=[here] * 4,
        out_specs=[pl.BlockSpec((rows, inner_width), lambda i: (i, 0)), here, far],
        out_shape=[
            pltpu.HBM((total, inner_width), F32),
            pltpu.VMEM((total, 4 * cells), BF16),
            pltpu.HBM((5, levels, (lon - 2) * lat), F32),
        ],
        scratch_shapes=[pltpu.VMEM((5, levels, (lon - 2) * lat), F32)]
        + scratch(lon)
        + [pltpu.SemaphoreType.DMA],
        compiler_params=params(),
        name="first_half_inner",
    )(*near_by(mix, east, north, field))

    ranges = pltpu.SMEM((2 * regions_of(capacity),), F32)
    own_w, own_e, rim_coef, weighted, place = pl.pallas_call(
        functools.partial(rim_kernel, lon=lon, levels=levels, tracers=tracers),
        in_specs=[here] * 6 + [far],
        out_specs=[here] * 5,
        out_shape=[
            pltpu.VMEM((total, cells), BF16),
            pltpu.VMEM((total, cells), BF16),
            pltpu.VMEM((5, levels, 4 * HALO * lat), F32),
            pltpu.VMEM((total, slots), BF16),
            pltpu.VMEM((8, slots), F32),
        ],
        scratch_shapes=scratch(6 * HALO, RIM_TOGETHER)
        + [
            ranges,
            pltpu.VMEM((total, 2 * cells), F32),
            pltpu.VMEM((bwd_rows, lat), BF16),
            pltpu.SemaphoreType.DMA,
        ],
        compiler_params=params(),
        name="rim",
    )(*near_by(mix, east, north, fwd, near, got), away(bwd))
    far_w = lax.ppermute(own_e, "tile", ring)
    far_e = lax.ppermute(own_w, "tile", back)
    inner = pl.pallas_call(
        functools.partial(forcing_inner_kernel, lat=lat),
        in_specs=[here] * 3,
        out_specs=here,
        out_shape=pltpu.VMEM((total, inner_width), BF16),
        scratch_shapes=[ranges, pltpu.VMEM((total, cells), F32)],
        compiler_params=params(),
        name="forcing_inner",
    )(*near_by(weighted, place, middle))

    out = pl.pallas_call(
        functools.partial(second_half_kernel, lon=lon, levels=levels),
        in_specs=[here] * 8,
        out_specs=far,
        out_shape=jax.ShapeDtypeStruct((total * lon, lat), F32),
        scratch_shapes=scratch(lon + 2 * HALO, TOGETHER)
        + [pltpu.VMEM((total * lon, lat), F32), pltpu.SemaphoreType.DMA((steps, levels // 8, GROUP))],
        compiler_params=params(),
        name="second_half",
    )(*near_by(mix, inner_coef, rim_coef, far_w, own_w, inner, own_e, far_e))
    return out.reshape(tracers, levels, lon, lat)


def solution(mesh):
    in_specs = (
        P("ens", None, "tile", None),
        P("ens", "tile", None),
        P("ens", "tile", None),
        P(),
        P("ens", "tile"),
        P("ens", "tile"),
        P("tile", "ens"),
        P("ens", "tile"),
    )
    out_specs = P("ens", None, "tile", None)
    return jax.shard_map(
        per_device, mesh=mesh, in_specs=in_specs, out_specs=out_specs, check_vma=False
    )
```
